32 devices in a mesh: grp: 4 (over z), seq: 8 (over y, x, core).
Axes of the slice: x: 2, y: 2, z: 4, core: 2. Of those that a mesh axis runs over, the one named last changes fastest.
Arguments:
- stream: bfloat16 [4096, 2048], P(('grp', 'seq')), may hold values from -64 to 64
- cotangent: bfloat16 [4096, 2048], P(('grp', 'seq')), may hold values from -6 to 6
- norm_gain: float32 [2048], replicated, may hold values from 0.5 to 1.5
- queries: bfloat16 [4096, 2048], P(('grp', 'seq')), may hold values from -6 to 6
- key_vectors: bfloat16 [4096, 2048], P(('grp', 'seq')), may hold values from -6 to 6
- value_vectors: bfloat16 [4096, 2048], P(('grp', 'seq')), may hold values from -6 to 6
- expert_index: int32 [32, 256], replicated, may hold values from 0 to 4095, as said below
- router_gates: float32 [32, 256], P(('grp', 'seq')), may hold values from 0.05 to 1
- gate_proj: bfloat16 [32, 2048, 768], P(('grp', 'seq')), may hold values from -0.125 to 0.125
- up_proj: bfloat16 [32, 2048, 768], P(('grp', 'seq')), may hold values from -0.125 to 0.125
- down_proj: bfloat16 [32, 768, 2048], P(('grp', 'seq')), may hold values from -0.21875 to 0.21875
Outputs:
- grad_stream: bfloat16 [4096, 2048], P(('grp', 'seq'))
- grad_queries: bfloat16 [4096, 2048], P(('grp', 'seq'))
- grad_keys: bfloat16 [4096, 2048], P(('grp', 'seq'))
- grad_values: bfloat16 [4096, 2048], P(('grp', 'seq'))
- grad_gate: bfloat16 [32, 2048, 768], P(('grp', 'seq'))
- grad_up: bfloat16 [32, 2048, 768], P(('grp', 'seq'))
- grad_down: bfloat16 [32, 768, 2048], P(('grp', 'seq'))
- grad_router: float32 [32, 256], P(('grp', 'seq'))
- grad_norm_gain: float32 [2048], replicated
The draws below stay inside these ranges and needn't reach their ends.
Inputs may be any that keep to these rules, and one draw needn't show every extreme that they name: `expert_index`: row e holds 256 different token numbers. Of the 128 tokens numbered d * 128 to (d + 1) * 128 - 1, one expert chooses at most 16, and in every row some d has exactly 16 chosen.
All inputs are finite; a program needn't handle non-finite values.
Results may differ from the reference program's by a relative error of at most 0.024.
Values may be sent and summed in bfloat16 or wider, within the bound.
No kernel may reach another device: no remote copies, remote signals or barrier semaphores. Data moves between devices by JAX's collectives and lax.ppermute only.
A program may use at most 192 MiB of HBM per device.

```python
import math
import jax
import jax.numpy as jnp
from jax import lax

D = 2048
FF = 768
HEADS = 16
HEAD = 128
CAP = 256
BLOCK = 128
T_DEV = 128
EXPERTS = 32
TOKENS = 4096
N_GRP = 4
N_SEQ = 8


def draw_stream(key, part):
    first, second = jax.random.split(key, 2)
    row_scale = jnp.exp(jax.random.uniform(second, (TOKENS, 1), jnp.float32) * math.log(10.0))
    base = jax.random.normal(first, (TOKENS, D), jnp.float32)
    return jnp.clip(base * row_scale, -64.0, 64.0).astype(jnp.bfloat16)


def choose_rows(expert_key):
    block_count = TOKENS // T_DEV
    half = block_count // 2
    base = CAP // block_count
    first, second, third, fourth = jax.random.split(expert_key, 4)
    shuffled = jax.random.permutation(first, block_count)
    delta = jax.random.randint(second, (half,), -base, base + 1)
    delta = delta.at[0].set(base)
    counts = jnp.full((block_count,), base, jnp.int32)
    counts = counts.at[shuffled[:half]].add(delta).at[shuffled[half:]].add(-delta)
    scores = jax.random.randint(third, (block_count, T_DEV), 0, 1 << 20) * T_DEV + jnp.arange(T_DEV)[None, :]
    ordering = jnp.argsort(scores, axis=1)
    ranking = jnp.argsort(ordering, axis=1)
    chosen = (ranking < counts[:, None]).reshape(-1)
    sort_key = jnp.where(chosen, 0, 1) * TOKENS + jnp.arange(TOKENS)
    picked = jnp.argsort(sort_key)[:CAP]
    mixing = jax.random.permutation(fourth, CAP)
    return picked[mixing].astype(jnp.int32)


def draw_expert_index(key, part):
    expert_keys = jax.random.split(jax.random.fold_in(key, 17), EXPERTS)
    return jax.vmap(choose_rows)(expert_keys).astype(jnp.int32)


def level_of(stream_key, shape, shards, least, top_value):
    factor_of = 1.0
    for dim, blocks in shards:
        steps = jax.random.uniform(jax.random.fold_in(jax.random.fold_in(stream_key, 6), dim), (blocks,), jnp.float32, least / len(shards), top_value / len(shards))
        factor_of = factor_of * jnp.repeat(jnp.exp(steps), shape[dim] // blocks).reshape((-1,) + (1,) * (len(shape) - 1 - dim))
    return factor_of


def bell_draw(rng, extent, scale, limit, pieces=(), held_as=jnp.bfloat16):
    level = level_of(rng, extent, pieces, -0.22, 0.18) if pieces else 1.0
    array = jax.random.normal(rng, extent, jnp.float32) * scale * level
    return jnp.minimum(jnp.maximum(array, -limit), limit).astype(held_as)


def setup_inputs(seed: int = 0) -> dict:
    key_of = jax.random.split(jax.random.key(seed), 12)
    return {
        "stream": draw_stream(jax.random.fold_in(key_of[11], 71), 0),
        "cotangent": bell_draw(key_of[1], (TOKENS, D), 1.0, 6.0, ((0, 32),)),
        "norm_gain": jnp.clip(1.0 + 0.1 * jax.random.normal(key_of[2], (D,), jnp.float32), 0.5, 1.5),
        "queries": bell_draw(key_of[3], (TOKENS, D), 1.0, 6.0, ((0, 32),)),
        "key_vectors": bell_draw(key_of[4], (TOKENS, D), 1.0, 6.0, ((0, 32),)),
        "value_vectors": bell_draw(key_of[5], (TOKENS, D), 1.0, 6.0, ((0, 32),)),
        "expert_index": draw_expert_index(jax.random.fold_in(key_of[11], 71), 0),
        "router_gates": jnp.clip(0.05 + 0.95 * jax.random.uniform(key_of[7], (EXPERTS, CAP), jnp.float32) ** level_of(key_of[7], (EXPERTS, CAP), ((0, 32),), -0.2, 0.2), 0.05, 1.0),
        "gate_proj": bell_draw(key_of[8], (EXPERTS, D, FF), D ** -0.5, 0.125, ((0, 32),)),
        "up_proj": bell_draw(key_of[9], (EXPERTS, D, FF), D ** -0.5, 0.125, ((0, 32),)),
        "down_proj": bell_draw(key_of[10], (EXPERTS, FF, D), FF ** -0.5, 0.21875, ((0, 32),)),
    }


EPS = 1e-06

def expert_back(rows, dy_rows, gates, w_gate, w_up, w_down):
    gate_pre = jnp.dot(rows, w_gate, preferred_element_type=jnp.float32)
    up_pre = jnp.dot(rows, w_up, preferred_element_type=jnp.float32)
    sigmoid_gate = jax.nn.sigmoid(gate_pre)
    silu_gate = gate_pre * sigmoid_gate
    hidden = (silu_gate * up_pre).astype(jnp.bfloat16)
    expert_out = jnp.dot(hidden, w_down, preferred_element_type=jnp.float32)
    grad_router = lax.optimization_barrier(jnp.sum(dy_rows.astype(jnp.float32) * expert_out, axis=1))
    grad_out = (gates[:, None] * dy_rows.astype(jnp.float32)).astype(jnp.bfloat16)
    grad_down = jnp.dot(hidden.T, grad_out, preferred_element_type=jnp.float32).astype(jnp.bfloat16)
    grad_hidden = jnp.dot(grad_out, w_down.T, preferred_element_type=jnp.float32)
    slope = sigmoid_gate * (1.0 + gate_pre * (1.0 - sigmoid_gate))
    grad_gate_pre = (grad_hidden * up_pre * slope).astype(jnp.bfloat16)
    grad_up_pre = (grad_hidden * silu_gate).astype(jnp.bfloat16)
    grad_gate = jnp.dot(rows.T, grad_gate_pre, preferred_element_type=jnp.float32).astype(jnp.bfloat16)
    grad_up = jnp.dot(rows.T, grad_up_pre, preferred_element_type=jnp.float32).astype(jnp.bfloat16)
    grad_rows = (jnp.dot(grad_gate_pre, w_gate.T, preferred_element_type=jnp.float32) + jnp.dot(grad_up_pre, w_up.T, preferred_element_type=jnp.float32)).astype(jnp.bfloat16)
    return (grad_rows, grad_gate, grad_up, grad_down, grad_router)

def rounded(values):
    return lax.optimization_barrier(values.astype(jnp.bfloat16)).astype(jnp.float32)

def reference(stream, cotangent, norm_gain, queries, key_vectors, value_vectors, expert_index, router_gates, gate_proj, up_proj, down_proj):
    wide_stream = stream.astype(jnp.float32)
    inverse_rms = lax.rsqrt(lax.optimization_barrier(jnp.mean(wide_stream * wide_stream, axis=1, keepdims=True)) + EPS)
    normed = wide_stream * inverse_rms
    inputs = (normed * norm_gain[None, :]).astype(jnp.bfloat16)

    def expert_step(accum, expert_item):
        chosen, gates, w_gate, w_up, w_down = expert_item
        grad_rows, grad_gate, grad_up, grad_down, grad_router = expert_back(inputs[chosen], cotangent[chosen], gates, w_gate, w_up, w_down)
        accum = accum.at[chosen].add(grad_rows.astype(jnp.float32))
        return (accum, (grad_gate, grad_up, grad_down, grad_router))
    start = jnp.zeros((TOKENS, D), jnp.float32)
    grad_inputs, (grad_gate, grad_up, grad_down, grad_router) = lax.scan(expert_step, start, (expert_index, router_gates, gate_proj, up_proj, down_proj))
    grad_norm_gain = lax.optimization_barrier(jnp.sum(grad_inputs * normed, axis=0))
    grad_normed = grad_inputs * norm_gain[None, :]
    grad_wide = cotangent.astype(jnp.float32) + inverse_rms * (grad_normed - normed * lax.optimization_barrier(jnp.mean(grad_normed * normed, axis=1, keepdims=True)))
    grad_stream = grad_wide.astype(jnp.bfloat16)
    blocks = T_DEV * N_SEQ // BLOCK
    scale = 1.0 / jnp.sqrt(jnp.float32(HEAD * T_DEV * N_SEQ))

    def shaped(values):
        return values.astype(jnp.float32).reshape(N_GRP, blocks, BLOCK, HEADS, HEAD)
    qq, kk, vv, gg = (shaped(queries), shaped(key_vectors), shaped(value_vectors), shaped(grad_stream))
    lower = jnp.arange(BLOCK)[:, None] >= jnp.arange(BLOCK)[None, :]
    high = lax.Precision.HIGHEST
    mix_a = rounded(jnp.where(lower, jnp.einsum('gntha,gnsha->gnhts', gg, vv, precision=high), 0.0))
    mix_b = rounded(jnp.where(lower, jnp.einsum('gntha,gnsha->gnhts', qq, kk, precision=high), 0.0))
    inc_state = jnp.einsum('gnsha,gnshb->gnhab', kk, vv, precision=high)
    inc_grad = jnp.einsum('gntha,gnthb->gnhab', qq, gg, precision=high)
    prior_state = jnp.cumsum(inc_state, axis=1) - inc_state
    later_state = jnp.cumsum(inc_grad[:, ::-1], axis=1)[:, ::-1] - inc_grad
    grad_q = scale * (jnp.einsum('gnhts,gnsha->gntha', mix_a, kk, precision=high) + jnp.einsum('gnthb,gnhab->gntha', gg, prior_state, precision=high))
    grad_k = scale * (jnp.einsum('gnhts,gntha->gnsha', mix_a, qq, precision=high) + jnp.einsum('gnshb,gnhab->gnsha', vv, later_state, precision=high))
    grad_v = scale * (jnp.einsum('gnhts,gnthb->gnshb', mix_b, gg, precision=high) + jnp.einsum('gnsha,gnhab->gnshb', kk, later_state, precision=high))
    grad_queries = grad_q.reshape(TOKENS, D).astype(jnp.bfloat16)
    grad_keys = grad_k.reshape(TOKENS, D).astype(jnp.bfloat16)
    grad_values = grad_v.reshape(TOKENS, D).astype(jnp.bfloat16)
    return (grad_stream, grad_queries, grad_keys, grad_values, grad_gate, grad_up, grad_down, grad_router, grad_norm_gain)
```

```python
import functools
import math

import jax
import jax.numpy as jnp
from jax import lax
from jax.experimental import pallas as pl
from jax.experimental.pallas import tpu as pltpu
from jax.sharding import PartitionSpec as P

HEAD = 128
EPS = 1e-06
F32 = jnp.float32
BF16 = jnp.bfloat16
AXES = ("grp", "seq")
VMEM_LIMIT = 63 * 1024 * 1024
CHUNK = 512

NN = (((1,), (0,)), ((), ()))
NT = (((1,), (1,)), ((), ()))
TN = (((0,), (0,)), ((), ()))


def mm(a, b, dims=NN):
    return lax.dot_general(a, b, dims, preferred_element_type=F32)


def params():
    return pltpu.CompilerParams(vmem_limit_bytes=VMEM_LIMIT)


def cost(flops, moved):
    return pl.CostEstimate(flops=flops, bytes_accessed=moved, transcendentals=0)


def pack_kernel(most, here_ref, index_ref, stream_ref, cot_ref, gain_ref, out_ref, pick_ref, inv_ref, member_ref):
    step = pl.program_id(0)
    tok, width = stream_ref.shape
    cap, experts = index_ref.shape
    rows, chunk = out_ref.shape
    x_steps = width // chunk

    @pl.when(step == 0)
    def _():
        wide = stream_ref[...].astype(F32)
        inv_ref[...] = lax.rsqrt(jnp.mean(wide * wide, axis=1, keepdims=True) + EPS)
        token = lax.broadcasted_iota(jnp.int32, (cap, tok), 1) + here_ref[0] * tok
        for e in range(experts):
            same = index_ref[:, e : e + 1] == token
            member_ref[e : e + 1, :] = jnp.sum(same.astype(F32), axis=0, keepdims=True)
        member = member_ref[...]
        before = lax.broadcasted_iota(jnp.int32, (tok, tok), 0) < lax.broadcasted_iota(jnp.int32, (tok, tok), 1)
        rank = mm(member.astype(BF16), before.astype(BF16))
        value = jnp.where(member > 0.0, rank, -1.0).astype(BF16)
        row = lax.broadcasted_iota(jnp.int32, (rows, experts), 0)
        first = lax.broadcasted_iota(jnp.int32, (rows, experts), 1) * most
        owner = (row >= first) & (row < first + most)
        spread = mm(owner.astype(BF16), value)
        place = jnp.sum(jnp.where(owner, row - first, 0), axis=1, keepdims=True)
        pick_ref[...] = (spread == place.astype(F32)).astype(BF16)

    @pl.when(step < x_steps)
    def _():
        at = pl.ds(pl.multiple_of(step * chunk, chunk), chunk)
        normed = stream_ref[:, at].astype(F32) * inv_ref[...]
        inputs = (normed * gain_ref[:, at]).astype(BF16)
        out_ref[...] = mm(pick_ref[...], inputs).astype(BF16)

    @pl.when(step >= x_steps)
    def _():
        at = pl.ds(pl.multiple_of((step - x_steps) * chunk, chunk), chunk)
        out_ref[...] = mm(pick_ref[...], cot_ref[:, at]).astype(BF16)


def pack(most, here, index_t, stream, cotangent, gain):
    tok, width = stream.shape
    cap, experts = index_t.shape
    rows = experts * most
    chunk = math.gcd(width, CHUNK)
    whole = lambda *shape: pl.BlockSpec(shape, lambda j: (0,) * len(shape))
    return pl.pallas_call(
        functools.partial(pack_kernel, most),
        grid=(2 * width // chunk,),
        in_specs=[
            pl.BlockSpec(memory_space=pltpu.SMEM),
            whole(cap, experts),
            whole(tok, width),
            whole(tok, width),
            whole(1, width),
        ],
        out_specs=[pl.BlockSpec((rows, chunk), lambda j: (0, j)), whole(rows, tok)],
        out_shape=[
            jax.ShapeDtypeStruct((rows, 2 * width), BF16),
            jax.ShapeDtypeStruct((rows, tok), BF16),
        ],
        scratch_shapes=[pltpu.VMEM((tok, 1), F32), pltpu.VMEM((experts, tok), F32)],
        compiler_params=params(),
        cost_estimate=cost(4 * rows * tok * width, 4 * rows * width),
        name="pack_rows",
    )(here, index_t, stream, cotangent, gain)


def columns(rows):
    return pl.BlockSpec((rows, CHUNK), lambda j: (0, j))


def states():
    return pl.BlockSpec((CHUNK // HEAD, HEAD, HEAD), lambda j: (j, 0, 0))


def heads_of(ref):
    return [slice(h * HEAD, (h + 1) * HEAD) for h in range(ref.shape[1] // HEAD)]


def early_kernel(q_ref, k_ref, v_ref, state_ref, mix_ref):
    tok = q_ref.shape[0]
    upper = lax.broadcasted_iota(jnp.int32, (tok, tok), 0) <= lax.broadcasted_iota(jnp.int32, (tok, tok), 1)
    for h, at in enumerate(heads_of(q_ref)):
        k = k_ref[:, at]
        state_ref[h] = mm(k, v_ref[:, at], TN).astype(BF16)
        mix_ref[:, at] = jnp.where(upper, mm(k, q_ref[:, at], NT), 0.0).astype(BF16)


def early(queries, keys, values):
    tok, width = queries.shape
    return pl.pallas_call(
        early_kernel,
        grid=(width // CHUNK,),
        in_specs=[columns(tok)] * 3,
        out_specs=[states(), columns(tok)],
        out_shape=[
            jax.ShapeDtypeStruct((width // HEAD, HEAD, HEAD), BF16),
            jax.ShapeDtypeStruct((tok, width), BF16),
        ],
        compiler_params=params(),
        cost_estimate=cost(4 * tok * HEAD * width, 10 * tok * width),
        name="early_states",
    )(queries, keys, values)


def combine_kernel(
    pick_ref, gain_ref, back_hbm, stream_hbm, cot_hbm, q_hbm, grad_ref, state_ref,
    back_ref, stream_ref, cot_ref, q_ref, sems,
):
    pairs = [(stream_hbm, stream_ref), (back_hbm, back_ref), (cot_hbm, cot_ref), (q_hbm, q_ref)]
    copies = [pltpu.make_async_copy(a, b, sems.at[i]) for i, (a, b) in enumerate(pairs)]
    for copy in copies:
        copy.start()
    copies[0].wait()
    wide = stream_ref[...].astype(F32)
    inv = lax.rsqrt(jnp.mean(wide * wide, axis=1, keepdims=True) + EPS)
    normed = wide * inv
    copies[1].wait()
    grad_normed = mm(pick_ref[...], back_ref[...]) * gain_ref[...]
    mean = jnp.mean(grad_normed * normed, axis=1, keepdims=True)
    copies[2].wait()
    grad = cot_ref[...].astype(F32) + inv * (grad_normed - normed * mean)
    grad_ref[...] = grad.astype(BF16)
    copies[3].wait()
    for h, at in enumerate(heads_of(q_ref)):
        state_ref[h] = mm(q_ref[:, at], grad_ref[:, at], TN).astype(BF16)


def combine(pick_t, back, stream, cotangent, gain, queries):
    tok, width = stream.shape
    vmem = pl.BlockSpec(memory_space=pltpu.VMEM)
    hbm = pl.BlockSpec(memory_space=pl.ANY)
    return pl.pallas_call(
        combine_kernel,
        in_specs=[vmem] * 2 + [hbm] * 4,
        out_specs=[vmem] * 2,
        out_shape=[
            jax.ShapeDtypeStruct((tok, width), BF16),
            jax.ShapeDtypeStruct((width // HEAD, HEAD, HEAD), BF16),
        ],
        scratch_shapes=[pltpu.VMEM(back.shape, BF16)]
        + [pltpu.VMEM((tok, width), BF16)] * 3
        + [pltpu.SemaphoreType.DMA((4,))],
        compiler_params=params(),
        cost_estimate=cost(2 * tok * width * (back.shape[0] + HEAD), 2 * width * (back.shape[0] + 6 * tok)),
        name="combine_rows",
    )(pick_t, gain, back, stream, cotangent, queries)


def expert_kernel(
    place_ref, place_t_ref, gates_ref, in_hbm, wg_hbm, wu_hbm, wd_hbm,
    back_hbm, table_hbm, rows_hbm, ggp_hbm, gup_hbm, hid_hbm, router_ref,
    in_ref, wg_ref, wu_ref, wd_ref, back_ref, table_ref, rows_ref, ggp_ref, gup_ref, hid_ref, sems,
):
    width = wg_ref.shape[0]
    steps = width // CHUNK
    count = iter(range(sems.shape[0]))
    pieces = [slice(j * CHUNK, (j + 1) * CHUNK) for j in range(2 * steps)]

    def copy(source, target):
        made = pltpu.make_async_copy(source, target, sems.at[next(count)])
        made.start()
        return made

    arrived = [copy(in_hbm.at[:, at], in_ref.at[:, at]) for at in pieces[:steps]]
    gate_in = copy(wg_hbm, wg_ref)
    up_in = copy(wu_hbm, wu_ref)
    arrived += [copy(in_hbm.at[:, at], in_ref.at[:, at]) for at in pieces[steps:]]
    down_in = copy(wd_hbm, wd_ref)
    place = place_ref[...]
    for at, part in zip(pieces[:steps], arrived):
        part.wait()
        table_ref[:, at] = mm(place, in_ref[:, at]).astype(BF16)
    rows = table_ref[:, :width]
    gate_in.wait()
    gate_pre = mm(rows, wg_ref[...])
    up_in.wait()
    up_pre = mm(rows, wu_ref[...])
    for at, part in zip(pieces[steps:], arrived[steps:]):
        part.wait()
        table_ref[:, at] = mm(place, in_ref[:, at]).astype(BF16)
    out = [copy(table_ref, table_hbm)]
    down_in.wait()
    raw_hidden = mm(table_ref[:, width:], wd_ref[...], NT)
    gates = gates_ref[...]
    sigmoid = 1.0 / (1.0 + jnp.exp(-gate_pre))
    silu = gate_pre * sigmoid
    hidden = silu * up_pre
    grad_hidden = gates * raw_hidden
    slope = sigmoid * (1.0 + gate_pre * (1.0 - sigmoid))
    ggp_ref[...] = (grad_hidden * up_pre * slope).astype(BF16)
    gup_ref[...] = (grad_hidden * silu).astype(BF16)
    out += [copy(ggp_ref, ggp_hbm), copy(gup_ref, gup_hbm)]
    place_t = place_t_ref[...]
    for at in pieces[:steps]:
        grad = mm(ggp_ref[...], wg_ref[at, :], NT) + mm(gup_ref[...], wu_ref[at, :], NT)
        rows_ref[:, at] = grad.astype(BF16)
        back_ref[:, at] = mm(place_t, rows_ref[:, at]).astype(BF16)
        out += [copy(back_ref.at[:, at], back_hbm.at[:, at])]
    hid_ref[...] = (hidden * gates).astype(BF16)
    router_ref[...] = jnp.sum(hidden.astype(BF16).astype(F32) * raw_hidden, axis=1, keepdims=True)
    out += [copy(hid_ref, hid_hbm), copy(rows_ref, rows_hbm)]
    for part in out:
        part.wait()


def expert(place, place_t, gates, incoming, w_gate, w_up, w_down):
    cap, slots = place.shape
    width, inner = w_gate.shape
    steps = width // CHUNK
    vmem = pl.BlockSpec(memory_space=pltpu.VMEM)
    hbm = pl.BlockSpec(memory_space=pl.ANY)
    results = [(slots, width), (cap, 2 * width), (cap, width), (cap, inner), (cap, inner), (cap, inner)]
    held = [incoming.shape, w_gate.shape, w_up.shape, w_down.shape] + results
    return pl.pallas_call(
        expert_kernel,
        in_specs=[vmem] * 3 + [hbm] * 4,
        out_specs=[hbm] * 6 + [vmem],
        out_shape=[jax.ShapeDtypeStruct(shape, BF16) for shape in results] + [jax.ShapeDtypeStruct((cap, 1), F32)],
        scratch_shapes=[pltpu.VMEM(shape, BF16) for shape in held] + [pltpu.SemaphoreType.DMA((3 * steps + 8,))],
        compiler_params=params(),
        cost_estimate=cost(10 * cap * width * inner + 6 * cap * slots * width, 2 * width * (3 * inner + 3 * slots)),
        name="expert_rows",
    )(place, place_t, gates, incoming, w_gate, w_up, w_down)


def total(value):
    count = lax.axis_size("grp") * lax.axis_size("seq")
    if count & (count - 1):
        return lax.psum(value, AXES)
    for b in range(count.bit_length() - 1):
        value = value + lax.ppermute(value, AXES, [(i, i ^ (1 << b)) for i in range(count)])
    return value


def local_kernel(scale, q_ref, k_ref, v_ref, g_ref, mix_ref, prior_ref, gq_ref, pk_ref, pv_ref):
    tok = q_ref.shape[0]
    row = lax.broadcasted_iota(jnp.int32, (tok, tok), 0)
    col = lax.broadcasted_iota(jnp.int32, (tok, tok), 1)
    for h, at in enumerate(heads_of(q_ref)):
        k, v, g = k_ref[:, at], v_ref[:, at], g_ref[:, at]
        mix_a = jnp.where(row >= col, mm(g, v, NT), 0.0).astype(BF16)
        mix_t = jnp.where(row <= col, mm(v, g, NT), 0.0).astype(BF16)
        gq_ref[:, at] = (scale * (mm(mix_a, k) + mm(g, prior_ref[h], NT))).astype(BF16)
        pk_ref[:, at] = mm(mix_t, q_ref[:, at])
        pv_ref[:, at] = mm(mix_ref[:, at], g)


def local_part(scale, queries, keys, values, grad, mix, prior):
    tok, width = queries.shape
    return pl.pallas_call(
        functools.partial(local_kernel, scale),
        grid=(width // CHUNK,),
        in_specs=[columns(tok)] * 5 + [states()],
        out_specs=[columns(tok)] * 3,
        out_shape=[
            jax.ShapeDtypeStruct((tok, width), BF16),
            jax.ShapeDtypeStruct((tok, width), F32),
            jax.ShapeDtypeStruct((tok, width), F32),
        ],
        compiler_params=params(),
        cost_estimate=cost(12 * tok * HEAD * width, 22 * tok * width),
        name="local_attention",
    )(queries, keys, values, grad, mix, prior)


def last_kernel(scale, k_ref, v_ref, pk_ref, pv_ref, later_ref, gk_ref, gv_ref):
    for h, at in enumerate(heads_of(k_ref)):
        later = later_ref[h]
        gk_ref[:, at] = (scale * (pk_ref[:, at] + mm(v_ref[:, at], later, NT))).astype(BF16)
        gv_ref[:, at] = (scale * (pv_ref[:, at] + mm(k_ref[:, at], later))).astype(BF16)


def last_part(scale, keys, values, pk, pv, later):
    tok, width = keys.shape
    return pl.pallas_call(
        functools.partial(last_kernel, scale),
        grid=(width // CHUNK,),
        in_specs=[columns(tok)] * 4 + [states()],
        out_specs=[columns(tok)] * 2,
        out_shape=[jax.ShapeDtypeStruct((tok, width), BF16)] * 2,
        compiler_params=params(),
        cost_estimate=cost(4 * tok * HEAD * width, 18 * tok * width),
        name="last_attention",
    )(keys, values, pk, pv, later)


def later_states(state):
    count = lax.axis_size("seq")
    place = lax.axis_index("seq")

    def swap(value, bit):
        return lax.ppermute(value.astype(BF16), "seq", [(i, i ^ bit) for i in range(count)]).astype(F32)

    if count & (count - 1) or count < 2 or state.shape[0] % 4:
        gathered = lax.all_gather(state, "seq")
        later = (jnp.arange(count) > place)[:, None, None, None]
        return jnp.sum(jnp.where(later, gathered.astype(F32), 0.0), axis=0).astype(BF16)
    bits = [1 << b for b in range(1, count.bit_length() - 1)]
    half = state.shape[0] // 2
    quarter = half // 2
    parity = place & 1
    parts = state.reshape((2, half) + state.shape[1:])
    mine = lax.dynamic_index_in_dim(parts, parity, 0, False)
    partner = swap(lax.dynamic_index_in_dim(parts, 1 - parity, 0, False), 1)
    mine = mine.astype(F32)
    both = mine + partner
    rising_sum, falling_base = both[:quarter], both[quarter:]
    rising = jnp.zeros_like(rising_sum)
    falling = jnp.zeros_like(falling_base)
    for up, down in zip(bits, reversed(bits)):
        got_up = swap(rising_sum, up)
        got_down = swap(falling + jnp.where((place & down) == 0, 0.0, falling_base), down)
        rising = rising + jnp.where((place & up) == 0, got_up, 0.0)
        rising_sum = rising_sum + got_up
        falling = falling + got_down
    beyond = jnp.concatenate([rising, falling])
    other = swap(beyond + jnp.where(parity == 1, mine, 0.0), 1).astype(BF16)
    own = (beyond + jnp.where(parity == 0, partner, 0.0)).astype(BF16)
    return jnp.concatenate([jnp.where(parity == 0, own, other), jnp.where(parity == 0, other, own)])


def body(
    stream,
    cotangent,
    norm_gain,
    queries,
    key_vectors,
    value_vectors,
    expert_index,
    router_gates,
    gate_proj,
    up_proj,
    down_proj,
):
    tok, width = stream.shape
    seq_count = lax.axis_size("seq")
    dev_count = seq_count * lax.axis_size("grp")
    experts, capacity = expert_index.shape
    most = 2 * capacity // dev_count
    here = lax.axis_index("grp") * seq_count + lax.axis_index("seq")
    scale = 1.0 / math.sqrt(HEAD * tok * seq_count)
    gain = norm_gain[None, :]
    w_gate, w_up, w_down = gate_proj[0], up_proj[0], down_proj[0]

    here_array = here.astype(jnp.int32)[None]
    outgoing, pick = pack(most, here_array, expert_index.T, stream, cotangent, gain)
    incoming = lax.all_to_all(outgoing, AXES, split_axis=0, concat_axis=0, tiled=True)

    key_state, mix_b = early(queries, key_vectors, value_vectors)
    gathered = lax.all_gather(key_state, "seq")
    pick_t = pick.T
    own_index = lax.dynamic_index_in_dim(expert_index, here, 0, keepdims=False)
    source = own_index // tok
    ahead = (source[None, :] == source[:, None]) & (own_index[None, :] < own_index[:, None])
    slot = source * most + jnp.sum(ahead.astype(jnp.int32), axis=1)
    place = (slot[:, None] == jnp.arange(dev_count * most)[None, :]).astype(BF16)
    place_t = (slot[None, :] == jnp.arange(dev_count * most)[:, None]).astype(BF16)
    gates = router_gates.reshape(capacity, 1)
    incoming, place, place_t, gates, mix_b, pick_t = lax.optimization_barrier(
        (incoming, place, place_t, gates, mix_b, pick_t)
    )

    back, table, grad_rows, grad_gate_pre, grad_up_pre, hidden, router = expert(
        place, place_t, gates, incoming, w_gate, w_up, w_down
    )
    returned = lax.all_to_all(back, AXES, split_axis=0, concat_axis=0, tiled=True)

    rows, dy_rows = table[:, :width], table[:, width:]
    gain_total = total((jnp.sum(grad_rows.astype(F32) * rows.astype(F32), axis=0) / norm_gain)[None, :])
    grad_gate = lax.dot_general(rows, grad_gate_pre, TN, preferred_element_type=F32).astype(BF16)
    grad_up = lax.dot_general(rows, grad_up_pre, TN, preferred_element_type=F32).astype(BF16)
    grad_down = lax.dot_general(hidden, dy_rows, TN, preferred_element_type=F32).astype(BF16)
    grad_router = router.reshape(1, capacity)
    earlier = (jnp.arange(seq_count) < lax.axis_index("seq"))[:, None, None, None]
    prior = jnp.sum(jnp.where(earlier, gathered.astype(F32), 0.0), axis=0).astype(BF16)
    returned, grad_gate, grad_up, grad_down, grad_router, prior, gain_total = lax.optimization_barrier(
        (returned, grad_gate, grad_up, grad_down, grad_router, prior, gain_total)
    )

    grad_stream, grad_state = combine(pick_t, returned, stream, cotangent, gain, queries)
    later = later_states(grad_state)
    grad_queries, part_k, part_v = local_part(
        scale, queries, key_vectors, value_vectors, grad_stream, mix_b, prior
    )
    grad_keys, grad_values = last_part(scale, key_vectors, value_vectors, part_k, part_v, later)
    return (
        grad_stream,
        grad_queries,
        grad_keys,
        grad_values,
        grad_gate[None],
        grad_up[None],
        grad_down[None],
        grad_router,
        gain_total[0],
    )


def solution(mesh):
    rows = P(AXES, None)
    cube = P(AXES, None, None)
    in_specs = (rows, rows, P(), rows, rows, rows, P(), rows, cube, cube, cube)
    out_specs = (rows, rows, rows, rows, cube, cube, cube, rows, P())
    return jax.shard_map(body, mesh=mesh, in_specs=in_specs, out_specs=out_specs, check_vma=False)
```

```python
import functools
import math

import jax
import jax.numpy as jnp
from jax import lax
from jax.experimental import pallas as pl
from jax.experimental.pallas import tpu as pltpu
from jax.sharding import PartitionSpec as P

HEAD = 128
EPS = 1e-06
F32 = jnp.float32
BF16 = jnp.bfloat16
AXES = ("grp", "seq")
VMEM_LIMIT = 63 * 1024 * 1024
TAIL_LIMIT = 63 * 1024 * 1024
CHUNK = 512

NN = (((1,), (0,)), ((), ()))
NT = (((1,), (1,)), ((), ()))
TN = (((0,), (0,)), ((), ()))


def mm(a, b, dims=NN):
    return lax.dot_general(a, b, dims, preferred_element_type=F32)


def params(limit=VMEM_LIMIT):
    return pltpu.CompilerParams(vmem_limit_bytes=limit)


def cost(flops, moved):
    return pl.CostEstimate(flops=flops, bytes_accessed=moved, transcendentals=0)


def one_hot_slots(most, device, index, member_ref, rows, tok):
    cap, experts = index.shape
    token = (lax.broadcasted_iota(jnp.int32, (cap, tok), 1) + device * tok).astype(F32)
    for e in range(experts):
        same = index[:, e : e + 1] == token
        member_ref[e : e + 1, :] = jnp.sum(same.astype(F32), axis=0, keepdims=True)
    member = member_ref[...]
    before = lax.broadcasted_iota(jnp.int32, (tok, tok), 0) < lax.broadcasted_iota(jnp.int32, (tok, tok), 1)
    rank = mm(member.astype(BF16), before.astype(BF16))
    value = jnp.where(member > 0.0, rank, -1.0).astype(BF16)
    row = lax.broadcasted_iota(jnp.int32, (rows, experts), 0)
    first = lax.broadcasted_iota(jnp.int32, (rows, experts), 1) * most
    owner = (row >= first) & (row < first + most)
    spread = mm(owner.astype(BF16), value)
    place = jnp.sum(jnp.where(owner, row - first, 0), axis=1, keepdims=True)
    return (spread == place.astype(F32)).astype(BF16)


def pick_kernel(most, device_ref, index_ref, pick_ref, member_ref):
    index = index_ref[...].astype(F32).T
    pick_ref[...] = one_hot_slots(most, device_ref[0], index, member_ref, *pick_ref.shape)


def picks(most, tok, device, index):
    experts, cap = index.shape
    return pl.pallas_call(
        functools.partial(pick_kernel, most),
        in_specs=[pl.BlockSpec(memory_space=pltpu.SMEM), pl.BlockSpec(memory_space=pltpu.VMEM)],
        out_specs=pl.BlockSpec(memory_space=pltpu.VMEM),
        out_shape=jax.ShapeDtypeStruct((experts * most, tok), BF16),
        scratch_shapes=[pltpu.VMEM((experts, tok), F32)],
        compiler_params=params(),
        cost_estimate=cost(1, 1),
        name="pick_slots",
    )(device, index)


def send_rows(pick_ref, sources, out_hbm, out_ref, sems):
    copies = []
    width = sources[0].shape[1]
    for i, source in enumerate(sources):
        for j in range(0, width, 2 * CHUNK):
            at = slice(i * width + j, i * width + j + 2 * CHUNK)
            out_ref[:, at] = mm(pick_ref[...], source[:, j : j + 2 * CHUNK]).astype(BF16)
            copies.append(pltpu.make_async_copy(out_ref.at[:, at], out_hbm.at[:, at], sems.at[len(copies)]))
            copies[-1].start()
    return copies


def prepare_kernel(
    most, half_ref, device_ref, index_ref, gain_ref, cot_ref, stream_ref, x_ref, out_hbm, out_ref, pick_ref, member_ref, sems
):
    del half_ref
    index = index_ref[...].astype(F32).T
    pick_ref[...] = one_hot_slots(most, device_ref[0], index, member_ref, *pick_ref.shape)
    wide = stream_ref[...].astype(F32)
    inv = lax.rsqrt(jnp.mean(wide * wide, axis=1, keepdims=True) + EPS)
    x_ref[...] = (wide * inv * gain_ref[...]).astype(BF16)
    for part in send_rows(pick_ref, (x_ref, cot_ref), out_hbm, out_ref, sems):
        part.wait()


def prepare(most, side, device, index, gain, cotangent, stream):
    tok, width = stream.shape
    experts, cap = index.shape
    experts = experts // 2
    rows = experts * most
    whole = lambda *shape: pl.BlockSpec(shape, lambda j, side: (0, 0))
    return pl.pallas_call(
        functools.partial(prepare_kernel, most),
        grid_spec=pltpu.PrefetchScalarGridSpec(
            num_scalar_prefetch=1,
            grid=(1,),
            in_specs=[
                pl.BlockSpec(memory_space=pltpu.SMEM),
                pl.BlockSpec((experts, cap), lambda j, side: (side[0], 0)),
                whole(1, width),
                whole(tok, width),
                whole(tok, width),
            ],
            out_specs=[whole(tok, width), pl.BlockSpec(memory_space=pl.ANY)],
            scratch_shapes=[
                pltpu.VMEM((rows, 2 * width), BF16),
                pltpu.VMEM((rows, tok), BF16),
                pltpu.VMEM((experts, tok), F32),
                pltpu.SemaphoreType.DMA((width // CHUNK,)),
            ],
        ),
        out_shape=[jax.ShapeDtypeStruct((tok, width), BF16), jax.ShapeDtypeStruct((rows, 2 * width), BF16)],
        compiler_params=params(),
        cost_estimate=cost(1, 1),
        name="prepare_rows",
    )(side, device, index, gain, cotangent, stream)


def pack_kernel(pick_ref, x_ref, cot_ref, out_hbm, out_ref, sems):
    for part in send_rows(pick_ref, (x_ref, cot_ref), out_hbm, out_ref, sems):
        part.wait()


def pack(pick, inputs, cotangent):
    width = inputs.shape[1]
    shape = (pick.shape[0], 2 * width)
    return pl.pallas_call(
        pack_kernel,
        in_specs=[pl.BlockSpec(memory_space=pltpu.VMEM)] * 3,
        out_specs=pl.BlockSpec(memory_space=pl.ANY),
        out_shape=jax.ShapeDtypeStruct(shape, BF16),
        scratch_shapes=[pltpu.VMEM(shape, BF16), pltpu.SemaphoreType.DMA((width // CHUNK,))],
        compiler_params=params(),
        cost_estimate=cost(1, 1),
        name="pack_rows",
    )(pick, inputs, cotangent)


def columns(rows):
    return pl.BlockSpec((rows, CHUNK), lambda j: (0, j))


def states():
    return pl.BlockSpec((CHUNK // HEAD, HEAD, HEAD), lambda j: (j, 0, 0))


def heads_of(ref):
    return [slice(h * HEAD, (h + 1) * HEAD) for h in range(ref.shape[1] // HEAD)]


def early_kernel(q_ref, k_ref, v_ref, state_ref, mix_ref):
    tok = q_ref.shape[0]
    upper = lax.broadcasted_iota(jnp.int32, (tok, tok), 0) <= lax.broadcasted_iota(jnp.int32, (tok, tok), 1)
    for h, at in enumerate(heads_of(q_ref)):
        k = k_ref[:, at]
        state_ref[h] = mm(k, v_ref[:, at], TN).astype(BF16)
        mix_ref[:, at] = jnp.where(upper, mm(k, q_ref[:, at], NT), 0.0).astype(BF16)


def early(queries, keys, values):
    tok, width = queries.shape
    return pl.pallas_call(
        early_kernel,
        grid=(width // CHUNK,),
        in_specs=[columns(tok)] * 3,
        out_specs=[states(), columns(tok)],
        out_shape=[
            jax.ShapeDtypeStruct((width // HEAD, HEAD, HEAD), BF16),
            jax.ShapeDtypeStruct((tok, width), BF16),
        ],
        compiler_params=params(),
        cost_estimate=cost(1, 1),
        name="early_states",
    )(queries, keys, values)


def combine_kernel(
    parity_ref, pick_ref, gain_ref, back_hbm, stream_hbm, cot_hbm, q_hbm, grad_ref, mine_ref, other_ref,
    back_ref, stream_ref, cot_ref, q_ref, sems,
):
    pairs = [(stream_hbm, stream_ref), (back_hbm, back_ref), (cot_hbm, cot_ref), (q_hbm, q_ref)]
    copies = [pltpu.make_async_copy(a, b, sems.at[i]) for i, (a, b) in enumerate(pairs)]
    for copy in copies:
        copy.start()
    copies[0].wait()
    wide = stream_ref[...].astype(F32)
    inv = lax.rsqrt(jnp.mean(wide * wide, axis=1, keepdims=True) + EPS)
    normed = wide * inv
    copies[1].wait()
    grad_normed = mm(pick_ref[...], back_ref[...]) * gain_ref[...]
    mean = jnp.mean(grad_normed * normed, axis=1, keepdims=True)
    copies[2].wait()
    grad = cot_ref[...].astype(F32) + inv * (grad_normed - normed * mean)
    grad_ref[...] = grad.astype(BF16)
    copies[3].wait()
    half = mine_ref.shape[0]
    for state_ref, first in ((other_ref, (1 - parity_ref[0]) * half), (mine_ref, parity_ref[0] * half)):
        for h in range(half):
            at = pl.ds(pl.multiple_of((first + h) * HEAD, HEAD), HEAD)
            state_ref[h] = mm(q_ref[:, at], grad_ref[:, at], TN).astype(BF16)


def combine(parity, pick_t, back, stream, cotangent, gain, queries):
    tok, width = stream.shape
    vmem = pl.BlockSpec(memory_space=pltpu.VMEM)
    hbm = pl.BlockSpec(memory_space=pl.ANY)
    return pl.pallas_call(
        combine_kernel,
        in_specs=[pl.BlockSpec(memory_space=pltpu.SMEM)] + [vmem] * 2 + [hbm] * 4,
        out_specs=[vmem] * 3,
        out_shape=[jax.ShapeDtypeStruct((tok, width), BF16)]
        + [jax.ShapeDtypeStruct((width // HEAD // 2, HEAD, HEAD), BF16)] * 2,
        scratch_shapes=[pltpu.VMEM(back.shape, BF16)]
        + [pltpu.VMEM((tok, width), BF16)] * 3
        + [pltpu.SemaphoreType.DMA((4,))],
        compiler_params=params(),
        cost_estimate=cost(2 * tok * width * (back.shape[0] + HEAD), 2 * width * (back.shape[0] + 6 * tok)),
        name="combine_rows",
    )(parity, pick_t, gain, back, stream, cotangent, queries)


def expert_kernel(
    place_ref, place_t_ref, gates_ref, own_hbm, far_hbm, wg_hbm, wu_hbm, wd_hbm,
    back_hbm, table_hbm, rows_hbm, ggp_hbm, gup_hbm, hid_hbm, router_ref,
    in_ref, wg_ref, wu_ref, wd_ref, back_ref, table_ref, rows_ref, ggp_ref, gup_ref, hid_ref, sems,
):
    width = wg_ref.shape[0]
    steps = width // CHUNK
    count = iter(range(sems.shape[0]))
    pieces = [slice(j * CHUNK, (j + 1) * CHUNK) for j in range(2 * steps)]

    def copy(source, target):
        made = pltpu.make_async_copy(source, target, sems.at[next(count)])
        made.start()
        return made

    near = own_hbm.shape[0]

    def fetch(at):
        first = copy(own_hbm.at[:, at], in_ref.at[:near, at])
        return first, copy(far_hbm.at[:, at], in_ref.at[near:, at])

    arrived = [fetch(at) for at in pieces[:steps]]
    gate_in = copy(wg_hbm, wg_ref)
    up_in = copy(wu_hbm, wu_ref)
    arrived += [fetch(at) for at in pieces[steps:]]
    down_in = copy(wd_hbm, wd_ref)
    place = place_ref[...]
    for at, part in zip(pieces[:steps], arrived):
        part[0].wait()
        part[1].wait()
        table_ref[:, at] = mm(place, in_ref[:, at]).astype(BF16)
    rows = table_ref[:, :width]
    gate_in.wait()
    gate_pre = mm(rows, wg_ref[...])
    up_in.wait()
    up_pre = mm(rows, wu_ref[...])
    for at, part in zip(pieces[steps:], arrived[steps:]):
        part[0].wait()
        part[1].wait()
        table_ref[:, at] = mm(place, in_ref[:, at]).astype(BF16)
    out = [copy(table_ref, table_hbm)]
    down_in.wait()
    raw_hidden = mm(table_ref[:, width:], wd_ref[...], NT)
    cap = place_ref.shape[0]
    same = lax.broadcasted_iota(jnp.int32, (cap, cap), 0) == lax.broadcasted_iota(jnp.int32, (cap, cap), 1)
    gates = jnp.sum(jnp.where(same, gates_ref[...], 0.0), axis=1, keepdims=True)
    sigmoid = 1.0 / (1.0 + jnp.exp(-gate_pre))
    silu = gate_pre * sigmoid
    hidden = silu * up_pre
    grad_hidden = gates * raw_hidden
    slope = sigmoid * (1.0 + gate_pre * (1.0 - sigmoid))
    ggp_ref[...] = (grad_hidden * up_pre * slope).astype(BF16)
    gup_ref[...] = (grad_hidden * silu).astype(BF16)
    out += [copy(ggp_ref, ggp_hbm), copy(gup_ref, gup_hbm)]
    place_t = place_t_ref[...]
    for at in pieces[:steps]:
        grad = mm(ggp_ref[...], wg_ref[at, :], NT) + mm(gup_ref[...], wu_ref[at, :], NT)
        rows_ref[:, at] = grad.astype(BF16)
        back_ref[:, at] = mm(place_t, rows_ref[:, at]).astype(BF16)
        out += [copy(back_ref.at[:, at], back_hbm.at[:, at])]
    hid_ref[...] = (hidden * gates).astype(BF16)
    router = jnp.sum(hidden.astype(BF16).astype(F32) * raw_hidden, axis=1, keepdims=True)
    router_ref[...] = jnp.sum(jnp.where(same, router, 0.0), axis=0, keepdims=True)
    out += [copy(hid_ref, hid_hbm), copy(rows_ref, rows_hbm)]
    for part in out:
        part.wait()


def expert(place, place_t, gates, own, far, w_gate, w_up, w_down):
    cap, slots = place.shape
    width, inner = w_gate.shape
    steps = width // CHUNK
    vmem = pl.BlockSpec(memory_space=pltpu.VMEM)
    hbm = pl.BlockSpec(memory_space=pl.ANY)
    results = [(slots, width), (cap, 2 * width), (cap, width), (cap, inner), (cap, inner), (cap, inner)]
    held = [(slots, 2 * width), w_gate.shape, w_up.shape, w_down.shape] + results
    return pl.pallas_call(
        expert_kernel,
        in_specs=[vmem] * 3 + [hbm] * 5,
        out_specs=[hbm] * 6 + [vmem],
        out_shape=[jax.ShapeDtypeStruct(shape, BF16) for shape in results] + [jax.ShapeDtypeStruct((1, cap), F32)],
        scratch_shapes=[pltpu.VMEM(shape, BF16) for shape in held] + [pltpu.SemaphoreType.DMA((5 * steps + 8,))],
        compiler_params=params(),
        cost_estimate=cost(10 * cap * width * inner + 6 * cap * slots * width, 2 * width * (3 * inner + 3 * slots)),
        name="expert_rows",
    )(place, place_t, gates, own, far, w_gate, w_up, w_down)


def total(value):
    count = lax.axis_size("grp") * lax.axis_size("seq")
    if count & (count - 1):
        return lax.psum(value, AXES)
    for b in range(count.bit_length() - 1):
        value = value + lax.ppermute(value, AXES, [(i, i ^ (1 << b)) for i in range(count)])
    return value


def local_kernel(scale, q_ref, k_ref, v_ref, g_ref, mix_ref, prior_ref, gq_ref, pk_ref, pv_ref):
    tok = q_ref.shape[0]
    row = lax.broadcasted_iota(jnp.int32, (tok, tok), 0)
    col = lax.broadcasted_iota(jnp.int32, (tok, tok), 1)
    for h, at in enumerate(heads_of(q_ref)):
        k, v, g = k_ref[:, at], v_ref[:, at], g_ref[:, at]
        mix_a = jnp.where(row >= col, mm(g, v, NT), 0.0).astype(BF16)
        mix_t = jnp.where(row <= col, mm(v, g, NT), 0.0).astype(BF16)
        gq_ref[:, at] = (scale * (mm(mix_a, k) + mm(g, prior_ref[h], NT))).astype(BF16)
        pk_ref[:, at] = mm(mix_t, q_ref[:, at])
        pv_ref[:, at] = mm(mix_ref[:, at], g)


def local_part(scale, queries, keys, values, grad, mix, prior):
    tok, width = queries.shape
    return pl.pallas_call(
        functools.partial(local_kernel, scale),
        grid=(width // CHUNK,),
        in_specs=[columns(tok)] * 5 + [states()],
        out_specs=[columns(tok)] * 3,
        out_shape=[
            jax.ShapeDtypeStruct((tok, width), BF16),
            jax.ShapeDtypeStruct((tok, width), F32),
            jax.ShapeDtypeStruct((tok, width), F32),
        ],
        compiler_params=params(),
        cost_estimate=cost(12 * tok * HEAD * width, 22 * tok * width),
        name="local_attention",
    )(queries, keys, values, grad, mix, prior)


def last_kernel(scale, split, parity_ref, k_ref, v_ref, pk_ref, pv_ref, own_ref, add_ref, other_ref, gk_ref, gv_ref):
    parity = parity_ref[0]
    is_own = (pl.program_id(0) >= split) == (parity == 1)
    for h, at in enumerate(heads_of(k_ref)):
        own = own_ref[h] + jnp.where(parity == 0, add_ref[h], 0.0)
        later = jnp.where(is_own, own.astype(BF16), other_ref[h])
        gk_ref[:, at] = (scale * (pk_ref[:, at] + mm(v_ref[:, at], later, NT))).astype(BF16)
        gv_ref[:, at] = (scale * (pv_ref[:, at] + mm(k_ref[:, at], later))).astype(BF16)


def last_part(scale, parity, keys, values, pk, pv, own, add, other):
    tok, width = keys.shape
    split = own.shape[0] * HEAD // CHUNK
    state = pl.BlockSpec((CHUNK // HEAD, HEAD, HEAD), lambda j: (lax.rem(j, split), 0, 0))
    return pl.pallas_call(
        functools.partial(last_kernel, scale, split),
        grid=(width // CHUNK,),
        in_specs=[pl.BlockSpec(memory_space=pltpu.SMEM)] + [columns(tok)] * 4 + [state] * 3,
        out_specs=[columns(tok)] * 2,
        out_shape=[jax.ShapeDtypeStruct((tok, width), BF16)] * 2,
        compiler_params=params(TAIL_LIMIT),
        cost_estimate=cost(4 * tok * HEAD * width, 18 * tok * width),
        name="last_attention",
    )(parity, keys, values, pk, pv, own, add, other)


def later_states(mine, other, beside):
    count = lax.axis_size("seq")
    place = lax.axis_index("seq")
    parity = place & 1

    def swap(value, bit):
        return lax.ppermute(value.astype(BF16), "seq", [(i, i ^ bit) for i in range(count)])

    bits = [1 << b for b in range(1, count.bit_length() - 1)]
    quarter = mine.shape[0] // 2
    partner = swap(other, 1).astype(F32)
    mine = mine.astype(F32)
    both = mine + partner
    rising_sum, falling_base = both[:quarter], both[quarter:]
    rising = jnp.zeros_like(rising_sum)
    falling = jnp.zeros_like(falling_base)
    beside_out = []
    for up, down in zip(bits, reversed(bits)):
        got_up = swap(rising_sum, up)
        got_down = swap(falling + jnp.where((place & down) == 0, 0.0, falling_base), down)
        if beside:
            got_up, got_down, done = lax.optimization_barrier((got_up, got_down, beside.pop(0)()))
            beside_out.append(done)
        got_up, got_down = got_up.astype(F32), got_down.astype(F32)
        rising = rising + jnp.where((place & up) == 0, got_up, 0.0)
        rising_sum = rising_sum + got_up
        falling = falling + got_down
    own = jnp.concatenate([rising, falling])
    theirs = swap(own + jnp.where(parity == 1, mine, 0.0), 1)
    return own, partner, theirs, beside_out + [work() for work in beside]


def body(
    stream,
    cotangent,
    norm_gain,
    queries,
    key_vectors,
    value_vectors,
    expert_index,
    router_gates,
    gate_proj,
    up_proj,
    down_proj,
):
    tok, width = stream.shape
    seq_count = lax.axis_size("seq")
    dev_count = seq_count * lax.axis_size("grp")
    experts, capacity = expert_index.shape
    most = 2 * capacity // dev_count
    here = lax.axis_index("grp") * seq_count + lax.axis_index("seq")
    scale = 1.0 / math.sqrt(HEAD * tok * seq_count)
    gain = norm_gain[None, :]
    w_gate, w_up, w_down = gate_proj[0], up_proj[0], down_proj[0]

    halves = dev_count // 2
    swap = [(i, (i + halves) % dev_count) for i in range(dev_count)]
    groups = [[side * halves + i for i in range(halves)] for side in range(2)]
    side = here // halves
    side_array = side.astype(jnp.int32)[None]
    parity = (lax.axis_index("seq") & 1).astype(jnp.int32)[None]
    here_array = here.astype(jnp.int32)[None]
    there_array = ((here + halves) % dev_count).astype(jnp.int32)[None]

    def exchange(value):
        return lax.all_to_all(value, AXES, split_axis=0, concat_axis=0, tiled=True, axis_index_groups=groups)

    inputs, out_own = prepare(most, side_array, here_array, expert_index, gain, cotangent, stream)
    own = exchange(out_own)
    far_cot = lax.ppermute(cotangent, AXES, swap)
    far_inputs = lax.ppermute(inputs, AXES, swap)

    key_state, mix_b = early(queries, key_vectors, value_vectors)
    gathered = lax.all_gather(key_state, "seq")
    pick_t = picks(most, tok, here_array, expert_index).T
    half_index = lax.dynamic_slice_in_dim(expert_index, side * (experts // 2), experts // 2, 0)
    far_pick = picks(most, tok, there_array, half_index)
    own_index = lax.dynamic_index_in_dim(expert_index, here, 0, keepdims=False)
    source = own_index // tok
    ahead = (source[None, :] == source[:, None]) & (own_index[None, :] < own_index[:, None])
    before = jnp.sum(ahead.astype(jnp.int32), axis=1)
    slot = source * most + before
    arrival = jnp.where(source // halves == side, source % halves, halves + source % halves) * most + before
    place = (arrival[:, None] == jnp.arange(dev_count * most)[None, :]).astype(BF16)
    place_t = (slot[None, :] == jnp.arange(dev_count * most)[:, None]).astype(BF16)
    far_cot, far_inputs, own, place, place_t, mix_b, pick_t, far_pick = lax.optimization_barrier(
        (far_cot, far_inputs, own, place, place_t, mix_b, pick_t, far_pick)
    )
    far = exchange(pack(far_pick, far_inputs, far_cot))

    back, table, grad_rows, grad_gate_pre, grad_up_pre, hidden, router = expert(
        place, place_t, router_gates, own, far, w_gate, w_up, w_down
    )
    returned = lax.all_to_all(back, AXES, split_axis=0, concat_axis=0, tiled=True)

    rows, dy_rows = table[:, :width], table[:, width:]
    gain_total = total((jnp.sum(grad_rows.astype(F32) * rows.astype(F32), axis=0) / norm_gain)[None, :])
    grad_gate = lax.dot_general(rows, grad_gate_pre, TN, preferred_element_type=F32).astype(BF16)
    grad_up = lax.dot_general(rows, grad_up_pre, TN, preferred_element_type=F32).astype(BF16)
    grad_down = lax.dot_general(hidden, dy_rows, TN, preferred_element_type=F32).astype(BF16)
    earlier = (jnp.arange(seq_count) < lax.axis_index("seq"))[:, None, None, None]
    prior = jnp.sum(jnp.where(earlier, gathered.astype(F32), 0.0), axis=0).astype(BF16)
    returned, grad_gate, grad_up, grad_down, router, prior, gain_total = lax.optimization_barrier(
        (returned, grad_gate, grad_up, grad_down, router, prior, gain_total)
    )

    grad_stream, mine, other = combine(parity, pick_t, returned, stream, cotangent, gain, queries)
    local = lambda: local_part(scale, queries, key_vectors, value_vectors, grad_stream, mix_b, prior)
    own_state, add_state, other_state, (done,) = later_states(mine, other, [local])
    grad_queries, part_k, part_v = done
    grad_keys, grad_values = last_part(
        scale, parity, key_vectors, value_vectors, part_k, part_v, own_state, add_state, other_state
    )
    return (
        grad_stream,
        grad_queries,
        grad_keys,
        grad_values,
        grad_gate[None],
        grad_up[None],
        grad_down[None],
        router,
        gain_total[0],
    )


def solution(mesh):
    rows = P(AXES, None)
    cube = P(AXES, None, None)
    in_specs = (rows, rows, P(), rows, rows, rows, P(), rows, cube, cube, cube)
    out_specs = (rows, rows, rows, rows, cube, cube, cube, rows, P())
    return jax.shard_map(body, mesh=mesh, in_specs=in_specs, out_specs=out_specs, check_vma=False)
```

```python
import functools
import math

import jax
import jax.numpy as jnp
from jax import lax
from jax.experimental import pallas as pl
from jax.experimental.pallas import tpu as pltpu
from jax.sharding import PartitionSpec as P

HEAD = 128
EPS = 1e-06
F32 = jnp.float32
BF16 = jnp.bfloat16
AXES = ("grp", "seq")
VMEM_LIMIT = 63 * 1024 * 1024
CHUNK = 512

NN = (((1,), (0,)), ((), ()))
NT = (((1,), (1,)), ((), ()))
TN = (((0,), (0,)), ((), ()))


def mm(a, b, dims=NN):
    return lax.dot_general(a, b, dims, preferred_element_type=F32)


def params():
    return pltpu.CompilerParams(vmem_limit_bytes=VMEM_LIMIT)


def cost(flops, moved):
    return pl.CostEstimate(flops=flops, bytes_accessed=moved, transcendentals=0)


def one_hot_slots(most, device, index, member_ref, rows, tok):
    cap, experts = index.shape
    token = (lax.broadcasted_iota(jnp.int32, (cap, tok), 1) + device * tok).astype(F32)
    for e in range(experts):
        same = index[:, e : e + 1] == token
        member_ref[e : e + 1, :] = jnp.sum(same.astype(F32), axis=0, keepdims=True)
    member = member_ref[...]
    before = lax.broadcasted_iota(jnp.int32, (tok, tok), 0) < lax.broadcasted_iota(jnp.int32, (tok, tok), 1)
    rank = mm(member.astype(BF16), before.astype(BF16))
    value = jnp.where(member > 0.0, rank, -1.0).astype(BF16)
    row = lax.broadcasted_iota(jnp.int32, (rows, experts), 0)
    first = lax.broadcasted_iota(jnp.int32, (rows, experts), 1) * most
    owner = (row >= first) & (row < first + most)
    spread = mm(owner.astype(BF16), value)
    place = jnp.sum(jnp.where(owner, row - first, 0), axis=1, keepdims=True)
    return (spread == place.astype(F32)).astype(BF16)


def pick_kernel(most, device_ref, index_ref, pick_ref, member_ref):
    index = index_ref[...].astype(F32).T
    pick_ref[...] = one_hot_slots(most, device_ref[0], index, member_ref, *pick_ref.shape)


def picks(most, tok, device, index):
    experts, cap = index.shape
    return pl.pallas_call(
        functools.partial(pick_kernel, most),
        in_specs=[pl.BlockSpec(memory_space=pltpu.SMEM), pl.BlockSpec(memory_space=pltpu.VMEM)],
        out_specs=pl.BlockSpec(memory_space=pltpu.VMEM),
        out_shape=jax.ShapeDtypeStruct((experts * most, tok), BF16),
        scratch_shapes=[pltpu.VMEM((experts, tok), F32)],
        compiler_params=params(),
        cost_estimate=cost(1, 1),
        name="pick_slots",
    )(device, index)


def send_rows(pick_ref, sources, out_hbm, out_ref, sems):
    copies = []
    width = sources[0].shape[1]
    for i, source in enumerate(sources):
        for j in range(0, width, 2 * CHUNK):
            at = slice(i * width + j, i * width + j + 2 * CHUNK)
            out_ref[:, at] = mm(pick_ref[...], source[:, j : j + 2 * CHUNK]).astype(BF16)
            copies.append(pltpu.make_async_copy(out_ref.at[:, at], out_hbm.at[:, at], sems.at[len(copies)]))
            copies[-1].start()
    return copies


def prepare_kernel(
    most, half_ref, device_ref, index_ref, gain_ref, cot_ref, stream_ref, x_ref, out_hbm, out_ref, pick_ref, member_ref, sems
):
    del half_ref
    index = index_ref[...].astype(F32).T
    pick_ref[...] = one_hot_slots(most, device_ref[0], index, member_ref, *pick_ref.shape)
    wide = stream_ref[...].astype(F32)
    inv = lax.rsqrt(jnp.mean(wide * wide, axis=1, keepdims=True) + EPS)
    x_ref[...] = (wide * inv * gain_ref[...]).astype(BF16)
    for part in send_rows(pick_ref, (x_ref, cot_ref), out_hbm, out_ref, sems):
        part.wait()


def prepare(most, side, device, index, gain, cotangent, stream):
    tok, width = stream.shape
    experts, cap = index.shape
    experts = experts // 2
    rows = experts * most
    whole = lambda *shape: pl.BlockSpec(shape, lambda j, side: (0, 0))
    return pl.pallas_call(
        functools.partial(prepare_kernel, most),
        grid_spec=pltpu.PrefetchScalarGridSpec(
            num_scalar_prefetch=1,
            grid=(1,),
            in_specs=[
                pl.BlockSpec(memory_space=pltpu.SMEM),
                pl.BlockSpec((experts, cap), lambda j, side: (side[0], 0)),
                whole(1, width),
                whole(tok, width),
                whole(tok, width),
            ],
            out_specs=[whole(tok, width), pl.BlockSpec(memory_space=pl.ANY)],
            scratch_shapes=[
                pltpu.VMEM((rows, 2 * width), BF16),
                pltpu.VMEM((rows, tok), BF16),
                pltpu.VMEM((experts, tok), F32),
                pltpu.SemaphoreType.DMA((width // CHUNK,)),
            ],
        ),
        out_shape=[jax.ShapeDtypeStruct((tok, width), BF16), jax.ShapeDtypeStruct((rows, 2 * width), BF16)],
        compiler_params=params(),
        cost_estimate=cost(1, 1),
        name="prepare_rows",
    )(side, device, index, gain, cotangent, stream)


def pack_kernel(pick_ref, x_ref, cot_ref, out_hbm, out_ref, sems):
    for part in send_rows(pick_ref, (x_ref, cot_ref), out_hbm, out_ref, sems):
        part.wait()


def pack(pick, inputs, cotangent):
    width = inputs.shape[1]
    shape = (pick.shape[0], 2 * width)
    return pl.pallas_call(
        pack_kernel,
        in_specs=[pl.BlockSpec(memory_space=pltpu.VMEM)] * 3,
        out_specs=pl.BlockSpec(memory_space=pl.ANY),
        out_shape=jax.ShapeDtypeStruct(shape, BF16),
        scratch_shapes=[pltpu.VMEM(shape, BF16), pltpu.SemaphoreType.DMA((width // CHUNK,))],
        compiler_params=params(),
        cost_estimate=cost(1, 1),
        name="pack_rows",
    )(pick, inputs, cotangent)


def streamed(work, name, scalar, ins, outs):
    width = max(x.shape[-1] for x in ins)
    steps = width // CHUNK
    group = CHUNK // HEAD

    def part(ref, j):
        if len(ref.shape) == 2:
            return ref.at[:, j * CHUNK : (j + 1) * CHUNK]
        return ref.at[j * group : (j + 1) * group]

    def kernel(*refs):
        scalar_ref, refs = refs[0], refs[1:]
        n, m = len(ins), len(outs)
        in_hbm, out_hbm, in_ref, out_ref = refs[:n], refs[n : n + m], refs[n + m : 2 * n + m], refs[2 * n + m : -1]
        count = iter(range(steps * (n + m)))

        def copy(source, target):
            made = pltpu.make_async_copy(source, target, refs[-1].at[next(count)])
            made.start()
            return made

        def used(ref):
            return [j for j in range(steps) if len(ref.shape) == 2 or j * group < ref.shape[0]]

        loads = [[] for _ in range(steps)]
        for j in range(steps):
            for a, b in zip(in_hbm, in_ref):
                if j in used(a):
                    loads[j].append(copy(part(a, j), part(b, j)))
        stores = []
        for j in range(steps):
            for load in loads[j]:
                load.wait()
            for h in range(j * group, (j + 1) * group):
                work(scalar_ref, h, slice(h * HEAD, (h + 1) * HEAD), in_ref, out_ref)
            stores += [copy(part(a, j), part(b, j)) for a, b in zip(out_ref, out_hbm) if len(a.shape) == 2]
        stores += [copy(a, b) for a, b in zip(out_ref, out_hbm) if len(a.shape) == 3]
        for store in stores:
            store.wait()

    hbm = pl.BlockSpec(memory_space=pl.ANY)
    return pl.pallas_call(
        kernel,
        in_specs=[pl.BlockSpec(memory_space=pltpu.SMEM)] + [hbm] * len(ins),
        out_specs=[hbm] * len(outs),
        out_shape=outs,
        scratch_shapes=[pltpu.VMEM(x.shape, x.dtype) for x in [*ins, *outs]]
        + [pltpu.SemaphoreType.DMA((steps * (len(ins) + len(outs)),))],
        compiler_params=params(),
        cost_estimate=cost(1, 1),
        name=name,
    )(scalar, *ins)


def triangle(tok):
    return lax.broadcasted_iota(jnp.int32, (tok, tok), 0), lax.broadcasted_iota(jnp.int32, (tok, tok), 1)


def early(parity, queries, keys, values):
    tok, width = queries.shape
    heads = width // HEAD

    def work(parity_ref, h, at, ins, outs):
        q_ref, k_ref, v_ref = ins
        state_ref, mix_ref = outs
        row, col = triangle(tok)
        k = k_ref[:, at]
        state_ref[lax.rem(h + parity_ref[0] * (heads // 2), heads)] = mm(k, v_ref[:, at], TN).astype(BF16)
        mix_ref[:, at] = jnp.where(row <= col, mm(k, q_ref[:, at], NT), 0.0).astype(BF16)

    states = jax.ShapeDtypeStruct((heads, HEAD, HEAD), BF16)
    outs = [states, jax.ShapeDtypeStruct((tok, width), BF16)]
    return streamed(work, "early_states", parity, [queries, keys, values], outs)


def combine_kernel(
    parity_ref, pick_ref, gain_ref, stream_hbm, back_hbm, cot_hbm, q_hbm, grad_hbm, mine_ref, other_ref,
    stream_ref, back_ref, cot_ref, q_ref, grad_ref, normed_ref, sum_ref, sems,
):
    width = stream_ref.shape[1]
    count = iter(range(sems.shape[0]))
    pieces = [slice(j, j + CHUNK) for j in range(0, width, CHUNK)]

    def copy(source, target):
        made = pltpu.make_async_copy(source, target, sems.at[next(count)])
        made.start()
        return made

    stream_in = copy(stream_hbm, stream_ref)
    back_in = [copy(back_hbm.at[:, at], back_ref.at[:, at]) for at in pieces]
    cot_in = copy(cot_hbm, cot_ref)
    q_in = copy(q_hbm, q_ref)
    stream_in.wait()
    wide = stream_ref[...].astype(F32)
    inv = lax.rsqrt(jnp.mean(wide * wide, axis=1, keepdims=True) + EPS)
    normed_ref[...] = wide * inv
    total = 0.0
    for part, at in zip(back_in, pieces):
        part.wait()
        grad_normed = mm(pick_ref[...], back_ref[:, at]) * gain_ref[:, at]
        sum_ref[:, at] = grad_normed
        total += jnp.sum(grad_normed * normed_ref[:, at], axis=1, keepdims=True)
    mean = total * (1.0 / width)
    cot_in.wait()
    for at in pieces:
        grad = cot_ref[:, at].astype(F32) + inv * (sum_ref[:, at] - normed_ref[:, at] * mean)
        grad_ref[:, at] = grad.astype(BF16)
    grad_out = copy(grad_ref, grad_hbm)
    q_in.wait()
    half = mine_ref.shape[0]
    for state_ref, first in ((other_ref, (1 - parity_ref[0]) * half), (mine_ref, parity_ref[0] * half)):
        for h in range(half):
            at = pl.ds(pl.multiple_of((first + h) * HEAD, HEAD), HEAD)
            state_ref[h] = mm(q_ref[:, at], grad_ref[:, at], TN).astype(BF16)
    grad_out.wait()


def combine(parity, pick_t, gain, stream, back, cotangent, queries):
    tok, width = stream.shape
    vmem = pl.BlockSpec(memory_space=pltpu.VMEM)
    hbm = pl.BlockSpec(memory_space=pl.ANY)
    return pl.pallas_call(
        combine_kernel,
        in_specs=[pl.BlockSpec(memory_space=pltpu.SMEM)] + [vmem] * 2 + [hbm] * 4,
        out_specs=[hbm] + [vmem] * 2,
        out_shape=[jax.ShapeDtypeStruct((tok, width), BF16)]
        + [jax.ShapeDtypeStruct((width // HEAD // 2, HEAD, HEAD), BF16)] * 2,
        scratch_shapes=[pltpu.VMEM((tok, width), BF16), pltpu.VMEM(back.shape, BF16)]
        + [pltpu.VMEM((tok, width), BF16)] * 3
        + [pltpu.VMEM((tok, width), F32)] * 2
        + [pltpu.SemaphoreType.DMA((width // CHUNK + 4,))],
        compiler_params=params(),
        cost_estimate=cost(2 * tok * width * (back.shape[0] + HEAD), 2 * width * (back.shape[0] + 6 * tok)),
        name="combine_rows",
    )(parity, pick_t, gain, stream, back, cotangent, queries)


def expert_kernel(
    first_ref, gates_ref, in_hbm, wg_hbm, wu_hbm, wd_hbm, _,
    back_hbm, ggp_hbm, gup_hbm, hid_hbm, router_ref, gain_ref,
    in_ref, wg_ref, wu_ref, wd_ref, back_ref, ggp_ref, gup_ref, hid_ref, sems,
):
    width = wg_ref.shape[0]
    slots = in_ref.shape[0]
    count = iter(range(sems.shape[0]))
    pieces = [slice(j, j + CHUNK) for j in range(0, width, CHUNK)]
    shifted = [slice(j, j + CHUNK) for j in range(width, 2 * width, CHUNK)]

    def copy(source, target):
        made = pltpu.make_async_copy(source, target, sems.at[next(count)])
        made.start()
        return made

    loads = []
    for at in pieces:
        loads += [copy(in_hbm.at[:, at], in_ref.at[:, at]), copy(wg_hbm.at[at, :], wg_ref.at[at, :])]
        loads += [copy(wu_hbm.at[at, :], wu_ref.at[at, :])]
    for at, there in zip(pieces, shifted):
        loads += [copy(in_hbm.at[:, there], in_ref.at[:, there]), copy(wd_hbm.at[:, at], wd_ref.at[:, at])]
    loads = iter(loads)
    gate_pre = up_pre = raw_hidden = 0.0
    for at in pieces:
        for _ in range(3):
            next(loads).wait()
        gate_pre += mm(in_ref[:, at], wg_ref[at, :])
        up_pre += mm(in_ref[:, at], wu_ref[at, :])
    for at, there in zip(pieces, shifted):
        for _ in range(2):
            next(loads).wait()
        raw_hidden += mm(in_ref[:, there], wd_ref[:, at], NT)
    same = lax.broadcasted_iota(jnp.int32, (slots, slots), 0) == lax.broadcasted_iota(jnp.int32, (slots, slots), 1)
    gates = jnp.sum(jnp.where(same, gates_ref[...], 0.0), axis=1, keepdims=True)
    sigmoid = 1.0 / (1.0 + jnp.exp(-gate_pre))
    silu = gate_pre * sigmoid
    hidden = silu * up_pre
    grad_hidden = gates * raw_hidden
    slope = sigmoid * (1.0 + gate_pre * (1.0 - sigmoid))
    ggp_ref[...] = (grad_hidden * up_pre * slope).astype(BF16)
    gup_ref[...] = (grad_hidden * silu).astype(BF16)
    out = [copy(ggp_ref, ggp_hbm), copy(gup_ref, gup_hbm)]
    hid_ref[...] = (hidden * gates).astype(BF16)
    router = jnp.sum(hidden.astype(BF16).astype(F32) * raw_hidden, axis=1, keepdims=True)
    router_ref[...] = jnp.sum(jnp.where(same, router, 0.0), axis=0, keepdims=True)
    out += [copy(hid_ref, hid_hbm)]
    first = pl.ds(pl.multiple_of(first_ref[0] * slots, slots), slots)
    for at in pieces:
        grad = mm(ggp_ref[...], wg_ref[at, :], NT) + mm(gup_ref[...], wu_ref[at, :], NT)
        back_ref[:, at] = grad.astype(BF16)
        out += [copy(back_ref.at[:, at], back_hbm.at[first, at])]
    for at in pieces:
        gain_ref[:, at] = jnp.sum(back_ref[:, at].astype(F32) * in_ref[:, at].astype(F32), axis=0, keepdims=True)
    for part in out:
        part.wait()


def expert(first, gates, incoming, w_gate, w_up, w_down, back=None):
    slots = incoming.shape[0]
    width, inner = w_gate.shape
    vmem = pl.BlockSpec(memory_space=pltpu.VMEM)
    hbm = pl.BlockSpec(memory_space=pl.ANY)
    small = [(slots, inner)] * 3
    held = [incoming.shape, w_gate.shape, w_up.shape, w_down.shape, (slots, width)] + small
    alias = {} if back is None else {6: 0}
    if back is None:
        back = gates
    return pl.pallas_call(
        expert_kernel,
        in_specs=[pl.BlockSpec(memory_space=pltpu.SMEM), vmem] + [hbm] * 5,
        out_specs=[hbm] * 4 + [vmem] * 2,
        out_shape=[jax.ShapeDtypeStruct(shape, BF16) for shape in [(2 * slots, width)] + small]
        + [jax.ShapeDtypeStruct((1, slots), F32), jax.ShapeDtypeStruct((1, width), F32)],
        scratch_shapes=[pltpu.VMEM(shape, BF16) for shape in held] + [pltpu.SemaphoreType.DMA((6 * width // CHUNK + 3,))],
        input_output_aliases=alias,
        compiler_params=params(),
        cost_estimate=cost(10 * slots * width * inner, 6 * width * (inner + slots)),
        name="expert_rows",
    )(first, gates, incoming, w_gate, w_up, w_down, back)


def total(value):
    count = lax.axis_size("grp") * lax.axis_size("seq")
    if count & (count - 1):
        return lax.psum(value, AXES)
    for b in range(count.bit_length() - 1):
        value = value + lax.ppermute(value, AXES, [(i, i ^ (1 << b)) for i in range(count)])
    return value


def local_part(scale, parity, queries, keys, values, grad, mix, prior):
    tok, width = queries.shape

    def work(_, h, at, ins, outs):
        q_ref, k_ref, v_ref, g_ref, mix_ref, prior_ref = ins
        gq_ref, pk_ref, pv_ref = outs
        row, col = triangle(tok)
        k, v, g = k_ref[:, at], v_ref[:, at], g_ref[:, at]
        mix_a = jnp.where(row >= col, mm(g, v, NT), 0.0).astype(BF16)
        mix_t = jnp.where(row <= col, mm(v, g, NT), 0.0).astype(BF16)
        gq_ref[:, at] = (scale * (mm(mix_a, k) + mm(g, prior_ref[h], NT))).astype(BF16)
        pk_ref[:, at] = mm(mix_t, q_ref[:, at]).astype(BF16)
        pv_ref[:, at] = mm(mix_ref[:, at], g).astype(BF16)

    outs = [jax.ShapeDtypeStruct((tok, width), BF16)] * 3
    return streamed(work, "local_attention", parity, [queries, keys, values, grad, mix, prior], outs)


def last_part(scale, parity, keys, values, pk, pv, own, other):
    tok, width = keys.shape
    half = own.shape[0]

    def work(parity_ref, h, at, ins, outs):
        k_ref, v_ref, pk_ref, pv_ref, own_ref, other_ref = ins
        gk_ref, gv_ref = outs
        later = jnp.where(parity_ref[0] == h // half, own_ref[h % half], other_ref[h % half])
        gk_ref[:, at] = (scale * (pk_ref[:, at].astype(F32) + mm(v_ref[:, at], later, NT))).astype(BF16)
        gv_ref[:, at] = (scale * (pv_ref[:, at].astype(F32) + mm(k_ref[:, at], later))).astype(BF16)

    outs = [jax.ShapeDtypeStruct((tok, width), BF16)] * 2
    return streamed(work, "last_attention", parity, [keys, values, pk, pv, own, other], outs)


def states_beyond(place, mine, other, beside):
    count = lax.axis_size("seq")
    parity = place & 1

    def swap(value, bit):
        return lax.ppermute(value.astype(BF16), "seq", [(i, i ^ bit) for i in range(count)])

    bits = [1 << b for b in range(1, count.bit_length() - 1)]
    quarter = mine.shape[0] // 2
    partner = swap(other, 1).astype(F32)
    mine = mine.astype(F32)
    both = mine + partner
    rising_sum, falling_base = both[:quarter], both[quarter:]
    rising = jnp.zeros_like(rising_sum)
    falling = jnp.zeros_like(falling_base)
    beside_out = None
    for up, down in zip(bits, reversed(bits)):
        got_up = swap(rising_sum, up)
        got_down = swap(falling + jnp.where((place & down) == 0, 0.0, falling_base), down)
        if beside is not None and beside_out is None:
            got_up, got_down, beside_out = lax.optimization_barrier((got_up, got_down, beside()))
        got_up, got_down = got_up.astype(F32), got_down.astype(F32)
        rising = rising + jnp.where((place & up) == 0, got_up, 0.0)
        rising_sum = rising_sum + got_up
        falling = falling + got_down
    own = jnp.concatenate([rising, falling])
    theirs = swap(own + jnp.where(parity == 1, mine, 0.0), 1)
    own = (own + jnp.where(parity == 0, partner, 0.0)).astype(BF16)
    return own, theirs, beside_out


def body(
    stream,
    cotangent,
    norm_gain,
    queries,
    key_vectors,
    value_vectors,
    expert_index,
    router_gates,
    gate_proj,
    up_proj,
    down_proj,
):
    tok, width = stream.shape
    seq_count = lax.axis_size("seq")
    dev_count = seq_count * lax.axis_size("grp")
    experts, capacity = expert_index.shape
    most = 2 * capacity // dev_count
    here = lax.axis_index("grp") * seq_count + lax.axis_index("seq")
    scale = 1.0 / math.sqrt(HEAD * tok * seq_count)
    gain = norm_gain[None, :]
    w_gate, w_up, w_down = gate_proj[0], up_proj[0], down_proj[0]

    halves = dev_count // 2
    swap = [(i, (i + halves) % dev_count) for i in range(dev_count)]
    groups = [[side * halves + i for i in range(halves)] for side in range(2)]
    side = here // halves
    side_array = side.astype(jnp.int32)[None]
    parity = (lax.axis_index("seq") & 1).astype(jnp.int32)[None]
    here_array = here.astype(jnp.int32)[None]
    there_array = ((here + halves) % dev_count).astype(jnp.int32)[None]

    def exchange(value):
        return lax.all_to_all(value, AXES, split_axis=0, concat_axis=0, tiled=True, axis_index_groups=groups)

    inputs, out_own = prepare(most, side_array, here_array, expert_index, gain, cotangent, stream)
    own = exchange(out_own)
    far_cot = lax.ppermute(cotangent, AXES, swap)
    far_inputs = lax.ppermute(inputs, AXES, swap)

    key_states, mix_b = early(parity, queries, key_vectors, value_vectors)
    heads = width // HEAD
    place = lax.axis_index("seq")
    own_prior, other_prior, _ = states_beyond(
        seq_count - 1 - place, key_states[: heads // 2], key_states[heads // 2 :], None
    )
    is_low = parity[0] == 0
    prior = jnp.concatenate(
        [jnp.where(is_low, own_prior, other_prior), jnp.where(is_low, other_prior, own_prior)]
    )
    pick_t = picks(most, tok, here_array, expert_index).T
    half_index = lax.dynamic_slice_in_dim(expert_index, side * (experts // 2), experts // 2, 0)
    far_pick = picks(most, tok, there_array, half_index)
    own_index = lax.dynamic_index_in_dim(expert_index, here, 0, keepdims=False)
    source = own_index // tok
    ahead = (source[None, :] == source[:, None]) & (own_index[None, :] < own_index[:, None])
    before = jnp.sum(ahead.astype(jnp.int32), axis=1)
    arrival = jnp.where(source // halves == side, source % halves, halves + source % halves) * most + before
    place_t = arrival[None, :] == jnp.arange(dev_count * most)[:, None]
    slot_gates = jnp.sum(jnp.where(place_t, router_gates, 0.0), axis=1).reshape(2, 1, halves * most)
    far_cot, far_inputs, mix_b, pick_t, far_pick, slot_gates, prior = lax.optimization_barrier(
        (far_cot, far_inputs, mix_b, pick_t, far_pick, slot_gates, prior)
    )
    far_out = pack(far_pick, far_inputs, far_cot)
    far = exchange(far_out)

    own, far_out = lax.optimization_barrier((own, far_out))
    back, own_ggp, own_gup, own_hidden, own_router, own_gain = expert(
        side_array, slot_gates[0], own, w_gate, w_up, w_down
    )
    far, back = lax.optimization_barrier((far, back))
    back, far_ggp, far_gup, far_hidden, far_router, far_gain = expert(
        1 - side_array, slot_gates[1], far, w_gate, w_up, w_down, back
    )
    returned = lax.all_to_all(back, AXES, split_axis=0, concat_axis=0, tiled=True)

    gain_total = total((own_gain + far_gain) / gain)
    own, far, far_ggp, back = lax.optimization_barrier((own, far, far_ggp, back))
    arrived = jnp.concatenate([own, far])
    rows, dy_rows = arrived[:, :width], arrived[:, width:]
    grad_gate_pre = jnp.concatenate([own_ggp, far_ggp])
    grad_up_pre = jnp.concatenate([own_gup, far_gup])
    hidden = jnp.concatenate([own_hidden, far_hidden])
    grad_gate = lax.dot_general(rows, grad_gate_pre, TN, preferred_element_type=F32).astype(BF16)
    grad_up = lax.dot_general(rows, grad_up_pre, TN, preferred_element_type=F32).astype(BF16)
    grad_down = lax.dot_general(hidden, dy_rows, TN, preferred_element_type=F32).astype(BF16)
    slot_router = jnp.concatenate([own_router, far_router], axis=1).reshape(dev_count * most, 1)
    router = jnp.sum(jnp.where(place_t, slot_router, 0.0), axis=0, keepdims=True)
    returned, grad_gate, grad_up, grad_down, router, gain_total = lax.optimization_barrier(
        (returned, grad_gate, grad_up, grad_down, router, gain_total)
    )

    grad_stream, mine, other = combine(parity, pick_t, gain, stream, returned, cotangent, queries)
    local = lambda: local_part(scale, parity, queries, key_vectors, value_vectors, grad_stream, mix_b, prior)
    own_state, other_state, done = states_beyond(place, mine, other, local)
    grad_queries, part_k, part_v = done
    grad_keys, grad_values = last_part(
        scale, parity, key_vectors, value_vectors, part_k, part_v, own_state, other_state
    )
    return (
        grad_stream,
        grad_queries,
        grad_keys,
        grad_values,
        grad_gate[None],
        grad_up[None],
        grad_down[None],
        router,
        gain_total[0],
    )


def solution(mesh):
    rows = P(AXES, None)
    cube = P(AXES, None, None)
    in_specs = (rows, rows, P(), rows, rows, rows, P(), rows, cube, cube, cube)
    out_specs = (rows, rows, rows, rows, cube, cube, cube, rows, P())
    return jax.shard_map(body, mesh=mesh, in_specs=in_specs, out_specs=out_specs, check_vma=False)
```

```python
import functools
import math

import jax
import jax.numpy as jnp
from jax import lax
from jax.experimental import pallas as pl
from jax.experimental.pallas import tpu as pltpu
from jax.sharding import PartitionSpec as P

HEAD = 128
EPS = 1e-06
F32 = jnp.float32
BF16 = jnp.bfloat16
AXES = ("grp", "seq")
VMEM_LIMIT = 63 * 1024 * 1024
CHUNK = 512

NN = (((1,), (0,)), ((), ()))
NT = (((1,), (1,)), ((), ()))
TN = (((0,), (0,)), ((), ()))


def mm(a, b, dims=NN):
    return lax.dot_general(a, b, dims, preferred_element_type=F32)


def params():
    return pltpu.CompilerParams(vmem_limit_bytes=VMEM_LIMIT)


def cost(flops, moved):
    return pl.CostEstimate(flops=flops, bytes_accessed=moved, transcendentals=0)


def one_hot_slots(most, device, index, member_ref, rows, tok):
    cap, experts = index.shape
    token = (lax.broadcasted_iota(jnp.int32, (cap, tok), 1) + device * tok).astype(F32)
    for e in range(experts):
        same = index[:, e : e + 1] == token
        member_ref[e : e + 1, :] = jnp.sum(same.astype(F32), axis=0, keepdims=True)
    member = member_ref[...]
    before = lax.broadcasted_iota(jnp.int32, (tok, tok), 0) < lax.broadcasted_iota(jnp.int32, (tok, tok), 1)
    rank = mm(member.astype(BF16), before.astype(BF16))
    value = jnp.where(member > 0.0, rank, -1.0).astype(BF16)
    row = lax.broadcasted_iota(jnp.int32, (rows, experts), 0)
    first = lax.broadcasted_iota(jnp.int32, (rows, experts), 1) * most
    owner = (row >= first) & (row < first + most)
    spread = mm(owner.astype(BF16), value)
    place = jnp.sum(jnp.where(owner, row - first, 0), axis=1, keepdims=True)
    return (spread == place.astype(F32)).astype(BF16)


def pick_kernel(most, device_ref, index_ref, pick_ref, member_ref):
    index = index_ref[...].astype(F32).T
    pick_ref[...] = one_hot_slots(most, device_ref[0], index, member_ref, *pick_ref.shape)


def picks(most, tok, device, index):
    experts, cap = index.shape
    return pl.pallas_call(
        functools.partial(pick_kernel, most),
        in_specs=[pl.BlockSpec(memory_space=pltpu.SMEM), pl.BlockSpec(memory_space=pltpu.VMEM)],
        out_specs=pl.BlockSpec(memory_space=pltpu.VMEM),
        out_shape=jax.ShapeDtypeStruct((experts * most, tok), BF16),
        scratch_shapes=[pltpu.VMEM((experts, tok), F32)],
        compiler_params=params(),
        cost_estimate=cost(1, 1),
        name="pick_slots",
    )(device, index)


def send_rows(pick_ref, sources, out_hbm, out_ref, sems):
    copies = []
    width = sources[0].shape[1]
    for i, source in enumerate(sources):
        for j in range(0, width, 2 * CHUNK):
            at = slice(i * width + j, i * width + j + 2 * CHUNK)
            out_ref[:, at] = mm(pick_ref[...], source[:, j : j + 2 * CHUNK]).astype(BF16)
            copies.append(pltpu.make_async_copy(out_ref.at[:, at], out_hbm.at[:, at], sems.at[len(copies)]))
            copies[-1].start()
    return copies


def prepare_kernel(
    most, half_ref, device_ref, index_hbm, gain_hbm, cot_hbm, stream_hbm, x_hbm, out_hbm,
    index_ref, gain_ref, cot_ref, stream_ref, x_ref, out_ref, pick_ref, member_ref, sems, edge_sems,
):
    half = index_ref.shape[0]
    first = pl.ds(pl.multiple_of(half_ref[0] * half, half), half)
    index_in = pltpu.make_async_copy(index_hbm.at[first, :], index_ref, edge_sems.at[3])
    gain_in = pltpu.make_async_copy(gain_hbm, gain_ref, edge_sems.at[4])
    index_in.start()
    gain_in.start()
    cot_in = pltpu.make_async_copy(cot_hbm, cot_ref, edge_sems.at[0])
    stream_in = pltpu.make_async_copy(stream_hbm, stream_ref, edge_sems.at[1])
    cot_in.start()
    stream_in.start()
    index_in.wait()
    index = index_ref[...].astype(F32).T
    pick_ref[...] = one_hot_slots(most, device_ref[0], index, member_ref, *pick_ref.shape)
    stream_in.wait()
    wide = stream_ref[...].astype(F32)
    inv = lax.rsqrt(jnp.mean(wide * wide, axis=1, keepdims=True) + EPS)
    gain_in.wait()
    x_ref[...] = (wide * inv * gain_ref[...]).astype(BF16)
    cot_in.wait()
    copies = send_rows(pick_ref, (x_ref, cot_ref), out_hbm, out_ref, sems)
    x_out = pltpu.make_async_copy(x_ref, x_hbm, edge_sems.at[2])
    x_out.start()
    for part in copies + [x_out]:
        part.wait()


def prepare(most, side, device, index, gain, cotangent, stream):
    tok, width = stream.shape
    experts, cap = index.shape
    experts = experts // 2
    rows = experts * most
    hbm = pl.BlockSpec(memory_space=pl.ANY)
    return pl.pallas_call(
        functools.partial(prepare_kernel, most),
        in_specs=[pl.BlockSpec(memory_space=pltpu.SMEM)] * 2 + [hbm] * 4,
        out_specs=[hbm] * 2,
        scratch_shapes=[pltpu.VMEM((experts, cap), jnp.int32), pltpu.VMEM((1, width), F32)]
        + [pltpu.VMEM((tok, width), BF16)] * 3
        + [
            pltpu.VMEM((rows, 2 * width), BF16),
            pltpu.VMEM((rows, tok), BF16),
            pltpu.VMEM((experts, tok), F32),
            pltpu.SemaphoreType.DMA((width // CHUNK,)),
            pltpu.SemaphoreType.DMA((5,)),
        ],
        out_shape=[jax.ShapeDtypeStruct((tok, width), BF16), jax.ShapeDtypeStruct((rows, 2 * width), BF16)],
        compiler_params=params(),
        cost_estimate=cost(1, 1),
        name="prepare_rows",
    )(side, device, index, gain, cotangent, stream)


def pack(pick, source, which, out=None):
    rows, width = pick.shape[0], source.shape[1]
    step = 2 * CHUNK

    def kernel(pick_hbm, source_hbm, _, out_hbm, pick_ref, source_ref, out_ref, sems):
        steps = width // step
        pick_in = pltpu.make_async_copy(pick_hbm, pick_ref, sems.at[2 * steps])
        pick_in.start()
        loads = []
        for j in range(0, width, step):
            at = slice(j, j + step)
            loads.append(pltpu.make_async_copy(source_hbm.at[:, at], source_ref.at[:, at], sems.at[steps + len(loads)]))
            loads[-1].start()
        pick_in.wait()
        copies = []
        for j in range(0, width, step):
            at = slice(j, j + step)
            loads[len(copies)].wait()
            out_ref[:, at] = mm(pick_ref[...], source_ref[:, at]).astype(BF16)
            there = out_hbm.at[:, which * width + j : which * width + j + step]
            copies.append(pltpu.make_async_copy(out_ref.at[:, at], there, sems.at[len(copies)]))
            copies[-1].start()
        for part in copies:
            part.wait()

    hbm = pl.BlockSpec(memory_space=pl.ANY)
    return pl.pallas_call(
        kernel,
        in_specs=[hbm] * 3,
        out_specs=hbm,
        out_shape=jax.ShapeDtypeStruct((rows, 2 * width), BF16),
        scratch_shapes=[
            pltpu.VMEM(pick.shape, BF16),
            pltpu.VMEM(source.shape, BF16),
            pltpu.VMEM((rows, width), BF16),
            pltpu.SemaphoreType.DMA((2 * width // step + 1,)),
        ],
        input_output_aliases={} if out is None else {2: 0},
        compiler_params=params(),
        cost_estimate=cost(1, 1),
        name="pack_rows",
    )(pick, source, source if out is None else out)


def streamed(work, name, scalar, ins, outs):
    width = max(x.shape[-1] for x in ins)
    steps = width // CHUNK
    group = CHUNK // HEAD

    def part(ref, j):
        if len(ref.shape) == 2:
            return ref.at[:, j * CHUNK : (j + 1) * CHUNK]
        return ref.at[j * group : (j + 1) * group]

    def kernel(*refs):
        scalar_ref, refs = refs[0], refs[1:]
        n, m = len(ins), len(outs)
        in_hbm, out_hbm, in_ref, out_ref = refs[:n], refs[n : n + m], refs[n + m : 2 * n + m], refs[2 * n + m : -1]
        count = iter(range(steps * (n + m)))

        def copy(source, target):
            made = pltpu.make_async_copy(source, target, refs[-1].at[next(count)])
            made.start()
            return made

        def used(ref):
            return [j for j in range(steps) if len(ref.shape) == 2 or j * group < ref.shape[0]]

        loads = [[] for _ in range(steps)]
        for j in range(steps):
            for a, b in zip(in_hbm, in_ref):
                if j in used(a):
                    loads[j].append(copy(part(a, j), part(b, j)))
        stores = []
        for j in range(steps):
            for load in loads[j]:
                load.wait()
            for h in range(j * group, (j + 1) * group):
                work(scalar_ref, h, slice(h * HEAD, (h + 1) * HEAD), in_ref, out_ref)
            stores += [copy(part(a, j), part(b, j)) for a, b in zip(out_ref, out_hbm) if len(a.shape) == 2]
        stores += [copy(a, b) for a, b in zip(out_ref, out_hbm) if len(a.shape) == 3]
        for store in stores:
            store.wait()

    hbm = pl.BlockSpec(memory_space=pl.ANY)
    return pl.pallas_call(
        kernel,
        in_specs=[pl.BlockSpec(memory_space=pltpu.SMEM)] + [hbm] * len(ins),
        out_specs=[hbm] * len(outs),
        out_shape=outs,
        scratch_shapes=[pltpu.VMEM(x.shape, x.dtype) for x in [*ins, *outs]]
        + [pltpu.SemaphoreType.DMA((steps * (len(ins) + len(outs)),))],
        compiler_params=params(),
        cost_estimate=cost(1, 1),
        name=name,
    )(scalar, *ins)


def triangle(tok):
    return lax.broadcasted_iota(jnp.int32, (tok, tok), 0), lax.broadcasted_iota(jnp.int32, (tok, tok), 1)


def early(parity, queries, keys, values):
    tok, width = queries.shape
    heads = width // HEAD

    def work(parity_ref, h, at, ins, outs):
        q_ref, k_ref, v_ref = ins
        state_ref, mix_ref = outs
        row, col = triangle(tok)
        k = k_ref[:, at]
        state_ref[lax.rem(h + parity_ref[0] * (heads // 2), heads)] = mm(k, v_ref[:, at], TN).astype(BF16)
        mix_ref[:, at] = jnp.where(row <= col, mm(k, q_ref[:, at], NT), 0.0).astype(BF16)

    states = jax.ShapeDtypeStruct((heads, HEAD, HEAD), BF16)
    outs = [states, jax.ShapeDtypeStruct((tok, width), BF16)]
    return streamed(work, "early_states", parity, [queries, keys, values], outs)


def combine_kernel(
    parity_ref, pick_hbm, gain_hbm, stream_hbm, back_hbm, cot_hbm, q_hbm, grad_hbm, mine_hbm, other_hbm,
    stream_ref, back_ref, cot_ref, q_ref, grad_ref, normed_ref, sum_ref, pick_ref, gain_ref, mine_ref, other_ref, sems,
):
    width = stream_ref.shape[1]
    count = iter(range(sems.shape[0]))
    pieces = [slice(j, j + CHUNK) for j in range(0, width, CHUNK)]

    def copy(source, target):
        made = pltpu.make_async_copy(source, target, sems.at[next(count)])
        made.start()
        return made

    stream_in = copy(stream_hbm, stream_ref)
    small_in = [copy(pick_hbm, pick_ref), copy(gain_hbm, gain_ref)]
    back_in = [copy(back_hbm.at[:, at], back_ref.at[:, at]) for at in pieces]
    cot_in = copy(cot_hbm, cot_ref)
    q_in = copy(q_hbm, q_ref)
    stream_in.wait()
    wide = stream_ref[...].astype(F32)
    inv = lax.rsqrt(jnp.mean(wide * wide, axis=1, keepdims=True) + EPS)
    normed_ref[...] = wide * inv
    for part in small_in:
        part.wait()
    total = 0.0
    for part, at in zip(back_in, pieces):
        part.wait()
        grad_normed = mm(pick_ref[...], back_ref[:, at]) * gain_ref[:, at]
        sum_ref[:, at] = grad_normed
        total += jnp.sum(grad_normed * normed_ref[:, at], axis=1, keepdims=True)
    mean = total * (1.0 / width)
    cot_in.wait()
    for at in pieces:
        grad = cot_ref[:, at].astype(F32) + inv * (sum_ref[:, at] - normed_ref[:, at] * mean)
        grad_ref[:, at] = grad.astype(BF16)
    out = [copy(grad_ref, grad_hbm)]
    q_in.wait()
    half = mine_ref.shape[0]
    sides = ((other_ref, other_hbm, (1 - parity_ref[0]) * half), (mine_ref, mine_hbm, parity_ref[0] * half))
    for state_ref, state_hbm, first in sides:
        for h in range(half):
            at = pl.ds(pl.multiple_of((first + h) * HEAD, HEAD), HEAD)
            state_ref[h] = mm(q_ref[:, at], grad_ref[:, at], TN).astype(BF16)
        out += [copy(state_ref, state_hbm)]
    for part in out:
        part.wait()


def combine(parity, pick_t, gain, stream, back, cotangent, queries):
    tok, width = stream.shape
    hbm = pl.BlockSpec(memory_space=pl.ANY)
    return pl.pallas_call(
        combine_kernel,
        in_specs=[pl.BlockSpec(memory_space=pltpu.SMEM)] + [hbm] * 6,
        out_specs=[hbm] * 3,
        out_shape=[jax.ShapeDtypeStruct((tok, width), BF16)]
        + [jax.ShapeDtypeStruct((width // HEAD // 2, HEAD, HEAD), BF16)] * 2,
        scratch_shapes=[pltpu.VMEM((tok, width), BF16), pltpu.VMEM(back.shape, BF16)]
        + [pltpu.VMEM((tok, width), BF16)] * 3
        + [pltpu.VMEM((tok, width), F32)] * 2
        + [pltpu.VMEM(pick_t.shape, BF16), pltpu.VMEM((1, width), F32)]
        + [pltpu.VMEM((width // HEAD // 2, HEAD, HEAD), BF16)] * 2
        + [pltpu.SemaphoreType.DMA((width // CHUNK + 8,))],
        compiler_params=params(),
        cost_estimate=cost(2 * tok * width * (back.shape[0] + HEAD), 2 * width * (back.shape[0] + 6 * tok)),
        name="combine_rows",
    )(parity, pick_t, gain, stream, back, cotangent, queries)


def expert_kernel(
    first_ref, gates_hbm, in_hbm, wg_hbm, wu_hbm, wd_hbm, _,
    back_hbm, ggp_hbm, gup_hbm, hid_hbm, router_hbm, gain_hbm,
    in_ref, wg_ref, wu_ref, wd_ref, back_ref, ggp_ref, gup_ref, hid_ref, gates_ref, router_ref, gain_ref, sems,
):
    width = wg_ref.shape[0]
    slots = in_ref.shape[0]
    count = iter(range(sems.shape[0]))
    pieces = [slice(j, j + CHUNK) for j in range(0, width, CHUNK)]
    shifted = [slice(j, j + CHUNK) for j in range(width, 2 * width, CHUNK)]

    def copy(source, target):
        made = pltpu.make_async_copy(source, target, sems.at[next(count)])
        made.start()
        return made

    loads = []
    for at in pieces:
        loads += [copy(in_hbm.at[:, at], in_ref.at[:, at]), copy(wg_hbm.at[at, :], wg_ref.at[at, :])]
        loads += [copy(wu_hbm.at[at, :], wu_ref.at[at, :])]
    for at, there in zip(pieces, shifted):
        loads += [copy(in_hbm.at[:, there], in_ref.at[:, there]), copy(wd_hbm.at[:, at], wd_ref.at[:, at])]
    gates_in = copy(gates_hbm, gates_ref)
    loads = iter(loads)
    gate_pre = up_pre = raw_hidden = 0.0
    for at in pieces:
        for _ in range(3):
            next(loads).wait()
        gate_pre += mm(in_ref[:, at], wg_ref[at, :])
        up_pre += mm(in_ref[:, at], wu_ref[at, :])
    for at, there in zip(pieces, shifted):
        for _ in range(2):
            next(loads).wait()
        raw_hidden += mm(in_ref[:, there], wd_ref[:, at], NT)
    same = lax.broadcasted_iota(jnp.int32, (slots, slots), 0) == lax.broadcasted_iota(jnp.int32, (slots, slots), 1)
    gates_in.wait()
    gates = jnp.sum(jnp.where(same, gates_ref[...], 0.0), axis=1, keepdims=True)
    sigmoid = 1.0 / (1.0 + jnp.exp(-gate_pre))
    silu = gate_pre * sigmoid
    hidden = silu * up_pre
    grad_hidden = gates * raw_hidden
    slope = sigmoid * (1.0 + gate_pre * (1.0 - sigmoid))
    ggp_ref[...] = (grad_hidden * up_pre * slope).astype(BF16)
    gup_ref[...] = (grad_hidden * silu).astype(BF16)
    out = [copy(ggp_ref, ggp_hbm), copy(gup_ref, gup_hbm)]
    hid_ref[...] = (hidden * gates).astype(BF16)
    router = jnp.sum(hidden.astype(BF16).astype(F32) * raw_hidden, axis=1, keepdims=True)
    router_ref[...] = jnp.sum(jnp.where(same, router, 0.0), axis=0, keepdims=True)
    out += [copy(hid_ref, hid_hbm), copy(router_ref, router_hbm)]
    first = pl.ds(pl.multiple_of(first_ref[0] * slots, slots), slots)
    for at in pieces:
        grad = mm(ggp_ref[...], wg_ref[at, :], NT) + mm(gup_ref[...], wu_ref[at, :], NT)
        back_ref[:, at] = grad.astype(BF16)
        out += [copy(back_ref.at[:, at], back_hbm.at[first, at])]
        gain_ref[:, at] = jnp.sum(back_ref[:, at].astype(F32) * in_ref[:, at].astype(F32), axis=0, keepdims=True)
    out += [copy(gain_ref, gain_hbm)]
    for part in out:
        part.wait()


def expert(first, gates, incoming, w_gate, w_up, w_down, back=None):
    slots = incoming.shape[0]
    width, inner = w_gate.shape
    hbm = pl.BlockSpec(memory_space=pl.ANY)
    small = [(slots, inner)] * 3
    held = [incoming.shape, w_gate.shape, w_up.shape, w_down.shape, (slots, width)] + small
    alias = {} if back is None else {6: 0}
    if back is None:
        back = gates
    return pl.pallas_call(
        expert_kernel,
        in_specs=[pl.BlockSpec(memory_space=pltpu.SMEM)] + [hbm] * 6,
        out_specs=[hbm] * 6,
        out_shape=[jax.ShapeDtypeStruct(shape, BF16) for shape in [(2 * slots, width)] + small]
        + [jax.ShapeDtypeStruct((1, slots), F32), jax.ShapeDtypeStruct((1, width), F32)],
        scratch_shapes=[pltpu.VMEM(shape, BF16) for shape in held]
        + [pltpu.VMEM((1, size), F32) for size in (slots, slots, width)]
        + [pltpu.SemaphoreType.DMA((6 * width // CHUNK + 6,))],
        input_output_aliases=alias,
        compiler_params=params(),
        cost_estimate=cost(10 * slots * width * inner, 6 * width * (inner + slots)),
        name="expert_rows",
    )(first, gates, incoming, w_gate, w_up, w_down, back)


def add_across(value, bit):
    count = lax.axis_size("grp") * lax.axis_size("seq")
    return value + lax.ppermute(value, AXES, [(i, i ^ bit) for i in range(count)])


def query_part(scale, parity, keys, values, grad, prior):
    tok, width = keys.shape

    def work(_, h, at, ins, outs):
        k_ref, v_ref, g_ref, prior_ref = ins
        row, col = triangle(tok)
        g = g_ref[:, at]
        mix_a = jnp.where(row >= col, mm(g, v_ref[:, at], NT), 0.0).astype(BF16)
        outs[0][:, at] = (scale * (mm(mix_a, k_ref[:, at]) + mm(g, prior_ref[h], NT))).astype(BF16)

    outs = [jax.ShapeDtypeStruct((tok, width), BF16)]
    return streamed(work, "query_attention", parity, [keys, values, grad, prior], outs)


def local_part(parity, queries, values, grad, mix):
    tok, width = queries.shape

    def work(_, h, at, ins, outs):
        q_ref, v_ref, g_ref, mix_ref = ins
        row, col = triangle(tok)
        g = g_ref[:, at]
        mix_t = jnp.where(row <= col, mm(v_ref[:, at], g, NT), 0.0).astype(BF16)
        outs[0][:, at] = mm(mix_t, q_ref[:, at]).astype(BF16)
        outs[1][:, at] = mm(mix_ref[:, at], g).astype(BF16)

    outs = [jax.ShapeDtypeStruct((tok, width), BF16)] * 2
    return streamed(work, "local_attention", parity, [queries, values, grad, mix], outs)


def last_part(scale, parity, keys, values, pk, pv, own, other):
    tok, width = keys.shape
    half = own.shape[0]

    def work(parity_ref, h, at, ins, outs):
        k_ref, v_ref, pk_ref, pv_ref, own_ref, other_ref = ins
        gk_ref, gv_ref = outs
        later = jnp.where(parity_ref[0] == h // half, own_ref[h % half], other_ref[h % half])
        gk_ref[:, at] = (scale * (pk_ref[:, at].astype(F32) + mm(v_ref[:, at], later, NT))).astype(BF16)
        gv_ref[:, at] = (scale * (pv_ref[:, at].astype(F32) + mm(k_ref[:, at], later))).astype(BF16)

    outs = [jax.ShapeDtypeStruct((tok, width), BF16)] * 2
    return streamed(work, "last_attention", parity, [keys, values, pk, pv, own, other], outs)


def states_beyond(place, mine, other, beside):
    count = lax.axis_size("seq")
    parity = place & 1

    def swap(value, bit):
        return lax.ppermute(value.astype(BF16), "seq", [(i, i ^ bit) for i in range(count)])

    bits = [1 << b for b in range(1, count.bit_length() - 1)]
    quarter = mine.shape[0] // 2
    partner = swap(other, 1).astype(F32)
    mine = mine.astype(F32)
    both = mine + partner
    rising_sum, falling_base = both[:quarter], both[quarter:]
    rising = jnp.zeros_like(rising_sum)
    falling = jnp.zeros_like(falling_base)
    beside_out = []
    for up, down in zip(bits, reversed(bits)):
        got_up = swap(rising_sum, up)
        got_down = swap(falling + jnp.where((place & down) == 0, 0.0, falling_base), down)
        if beside:
            got_up, got_down, done = lax.optimization_barrier((got_up, got_down, beside.pop(0)(rising_sum)))
            beside_out.append(done)
        got_up, got_down = got_up.astype(F32), got_down.astype(F32)
        rising = rising + jnp.where((place & up) == 0, got_up, 0.0)
        rising_sum = rising_sum + got_up
        falling = falling + got_down
    own = jnp.concatenate([rising, falling])
    theirs = swap(own + jnp.where(parity == 1, mine, 0.0), 1)
    own = (own + jnp.where(parity == 0, partner, 0.0)).astype(BF16)
    return own, theirs, beside_out + [work(rising_sum) for work in beside]


def body(
    stream,
    cotangent,
    norm_gain,
    queries,
    key_vectors,
    value_vectors,
    expert_index,
    router_gates,
    gate_proj,
    up_proj,
    down_proj,
):
    tok, width = stream.shape
    seq_count = lax.axis_size("seq")
    dev_count = seq_count * lax.axis_size("grp")
    experts, capacity = expert_index.shape
    most = 2 * capacity // dev_count
    here = lax.axis_index("grp") * seq_count + lax.axis_index("seq")
    scale = 1.0 / math.sqrt(HEAD * tok * seq_count)
    gain = norm_gain[None, :]
    w_gate, w_up, w_down = gate_proj[0], up_proj[0], down_proj[0]

    halves = dev_count // 2
    swap = [(i, (i + halves) % dev_count) for i in range(dev_count)]
    groups = [[side * halves + i for i in range(halves)] for side in range(2)]
    side = here // halves
    side_array = side.astype(jnp.int32)[None]
    parity = (lax.axis_index("seq") & 1).astype(jnp.int32)[None]
    here_array = here.astype(jnp.int32)[None]
    there_array = ((here + halves) % dev_count).astype(jnp.int32)[None]

    def exchange(value):
        return lax.all_to_all(value, AXES, split_axis=0, concat_axis=0, tiled=True, axis_index_groups=groups)

    inputs, out_own = prepare(most, side_array, here_array, expert_index, gain, cotangent, stream)
    own = exchange(out_own)
    far_cot = lax.ppermute(cotangent, AXES, swap)
    far_inputs = lax.ppermute(inputs, AXES, swap)

    pick_t = picks(most, tok, here_array, expert_index).T
    half_index = lax.dynamic_slice_in_dim(expert_index, side * (experts // 2), experts // 2, 0)
    far_pick = picks(most, tok, there_array, half_index)
    own_index = lax.dynamic_index_in_dim(expert_index, here, 0, keepdims=False)
    source = own_index // tok
    ahead = (source[None, :] == source[:, None]) & (own_index[None, :] < own_index[:, None])
    before = jnp.sum(ahead.astype(jnp.int32), axis=1)
    arrival = jnp.where(source // halves == side, source % halves, halves + source % halves) * most + before
    place_t = arrival[None, :] == jnp.arange(dev_count * most)[:, None]
    slot_gates = jnp.sum(jnp.where(place_t, router_gates, 0.0), axis=1).reshape(2, 1, halves * most)
    far_out = pack(far_pick, far_cot, 1)
    far_inputs, far_out, pick_t, slot_gates = lax.optimization_barrier((far_inputs, far_out, pick_t, slot_gates))
    far_out = pack(far_pick, far_inputs, 0, far_out)
    far = exchange(far_out)

    own, far_out, q_early, k_early, v_early = lax.optimization_barrier(
        (own, far_out, queries, key_vectors, value_vectors)
    )
    key_states, mix_b = early(parity, q_early, k_early, v_early)
    back, own_ggp, own_gup, own_hidden, own_router, own_gain = expert(
        side_array, slot_gates[0], own, w_gate, w_up, w_down
    )
    far, back, key_states, mix_b = lax.optimization_barrier((far, back, key_states, mix_b))
    back, far_ggp, far_gup, far_hidden, far_router, far_gain = expert(
        1 - side_array, slot_gates[1], far, w_gate, w_up, w_down, back
    )
    returned = lax.all_to_all(back, AXES, split_axis=0, concat_axis=0, tiled=True)

    heads = width // HEAD
    place = lax.axis_index("seq")
    own_prior, other_prior, _ = states_beyond(
        seq_count - 1 - place, key_states[: heads // 2], key_states[heads // 2 :], []
    )
    is_low = parity[0] == 0
    prior = jnp.concatenate(
        [jnp.where(is_low, own_prior, other_prior), jnp.where(is_low, other_prior, own_prior)]
    )
    own, far, far_ggp, back = lax.optimization_barrier((own, far, far_ggp, back))
    arrived = jnp.concatenate([own, far])
    arrived, own_gain, far_gain = lax.optimization_barrier((arrived, own_gain, far_gain))
    gain_total = (own_gain + far_gain) / gain
    bits = [1 << b for b in range(dev_count.bit_length() - 1)]
    for bit in bits[:-2]:
        gain_total = add_across(gain_total, bit)
    rows, dy_rows = arrived[:, :width], arrived[:, width:]
    grad_gate_pre = jnp.concatenate([own_ggp, far_ggp])
    grad_up_pre = jnp.concatenate([own_gup, far_gup])
    hidden = jnp.concatenate([own_hidden, far_hidden])
    grad_gate = lax.dot_general(rows, grad_gate_pre, TN, preferred_element_type=F32).astype(BF16)
    grad_up = lax.dot_general(rows, grad_up_pre, TN, preferred_element_type=F32).astype(BF16)
    grad_down = lax.dot_general(hidden, dy_rows, TN, preferred_element_type=F32).astype(BF16)
    slot_router = jnp.concatenate([own_router, far_router], axis=1).reshape(dev_count * most, 1)
    router = jnp.sum(jnp.where(place_t, slot_router, 0.0), axis=0, keepdims=True)
    returned, grad_gate, grad_up, grad_down, router, gain_total, prior, mix_b = lax.optimization_barrier(
        (returned, grad_gate, grad_up, grad_down, router, gain_total, prior, mix_b)
    )

    grad_stream, mine, other = combine(parity, pick_t, gain, stream, returned, cotangent, queries)

    gain_across = [(i, i ^ bits[-1]) for i in range(dev_count)]
    gain_sums = [gain_total]

    def first(_):
        gain_sums.append(add_across(gain_total, bits[-2]))
        return local_part(parity, queries, value_vectors, grad_stream, mix_b), gain_sums[-1]

    def second(after):
        grad, _ = lax.optimization_barrier((grad_stream, after))
        done = query_part(scale, parity, key_vectors, value_vectors, grad, prior)
        return done, lax.ppermute(gain_sums[-1], AXES, gain_across)

    own_state, other_state, done = states_beyond(place, mine, other, [first, second])
    ((part_k, part_v), gain_total), ((grad_queries,), gain_other) = done
    gain_total += gain_other
    grad_keys, grad_values = last_part(
        scale, parity, key_vectors, value_vectors, part_k, part_v, own_state, other_state
    )
    return (
        grad_stream,
        grad_queries,
        grad_keys,
        grad_values,
        grad_gate[None],
        grad_up[None],
        grad_down[None],
        router,
        gain_total[0],
    )


def solution(mesh):
    rows = P(AXES, None)
    cube = P(AXES, None, None)
    in_specs = (rows, rows, P(), rows, rows, rows, P(), rows, cube, cube, cube)
    out_specs = (rows, rows, rows, rows, cube, cube, cube, rows, P())
    return jax.shard_map(body, mesh=mesh, in_specs=in_specs, out_specs=out_specs, check_vma=False)
```

```python
import functools
import math

import jax
import jax.numpy as jnp
from jax import lax
from jax.experimental import pallas as pl
from jax.experimental.pallas import tpu as pltpu
from jax.sharding import PartitionSpec as P

HEAD = 128
EPS = 1e-06
F32 = jnp.float32
BF16 = jnp.bfloat16
AXES = ("grp", "seq")
VMEM_LIMIT = 63 * 1024 * 1024
CHUNK = 512
WIDE = 1024

NN = (((1,), (0,)), ((), ()))
NT = (((1,), (1,)), ((), ()))
TN = (((0,), (0,)), ((), ()))


def mm(a, b, dims=NN):
    return lax.dot_general(a, b, dims, preferred_element_type=F32)


def params():
    return pltpu.CompilerParams(vmem_limit_bytes=VMEM_LIMIT)


def cost(flops, moved):
    return pl.CostEstimate(flops=flops, bytes_accessed=moved, transcendentals=0)


def one_hot_slots(most, device, index, member_ref, rows, tok):
    cap, experts = index.shape
    token = (lax.broadcasted_iota(jnp.int32, (cap, tok), 1) + device * tok).astype(F32)
    for e in range(experts):
        same = index[:, e : e + 1] == token
        member_ref[e : e + 1, :] = jnp.sum(same.astype(F32), axis=0, keepdims=True)
    member = member_ref[...]
    before = lax.broadcasted_iota(jnp.int32, (tok, tok), 0) < lax.broadcasted_iota(jnp.int32, (tok, tok), 1)
    rank = mm(member.astype(BF16), before.astype(BF16))
    value = jnp.where(member > 0.0, rank, -1.0).astype(BF16)
    row = lax.broadcasted_iota(jnp.int32, (rows, experts), 0)
    first = lax.broadcasted_iota(jnp.int32, (rows, experts), 1) * most
    owner = (row >= first) & (row < first + most)
    spread = mm(owner.astype(BF16), value)
    place = jnp.sum(jnp.where(owner, row - first, 0), axis=1, keepdims=True)
    return (spread == place.astype(F32)).astype(BF16)


def pick_kernel(most, device_ref, index_ref, pick_ref, member_ref):
    index = index_ref[...].astype(F32).T
    pick_ref[...] = one_hot_slots(most, device_ref[0], index, member_ref, *pick_ref.shape)


def picks(most, tok, device, index):
    experts, cap = index.shape
    return pl.pallas_call(
        functools.partial(pick_kernel, most),
        in_specs=[pl.BlockSpec(memory_space=pltpu.SMEM), pl.BlockSpec(memory_space=pltpu.VMEM)],
        out_specs=pl.BlockSpec(memory_space=pltpu.VMEM),
        out_shape=jax.ShapeDtypeStruct((experts * most, tok), BF16),
        scratch_shapes=[pltpu.VMEM((experts, tok), F32)],
        compiler_params=params(),
        cost_estimate=cost(1, 1),
        name="pick_slots",
    )(device, index)


def send_rows(pick_ref, sources, out_hbm, out_ref, sems):
    copies = []
    width = sources[0].shape[1]
    for i, source in enumerate(sources):
        for j in range(0, width, 2 * CHUNK):
            at = slice(i * width + j, i * width + j + 2 * CHUNK)
            out_ref[:, at] = mm(pick_ref[...], source[:, j : j + 2 * CHUNK]).astype(BF16)
            copies.append(pltpu.make_async_copy(out_ref.at[:, at], out_hbm.at[:, at], sems.at[len(copies)]))
            copies[-1].start()
    return copies


def prepare_kernel(
    most, half_ref, device_ref, index_hbm, gain_hbm, cot_hbm, stream_hbm, x_hbm, out_hbm,
    index_ref, gain_ref, cot_ref, stream_ref, x_ref, out_ref, pick_ref, member_ref, sems, edge_sems,
):
    half = index_ref.shape[0]
    first = pl.ds(pl.multiple_of(half_ref[0] * half, half), half)
    index_in = pltpu.make_async_copy(index_hbm.at[first, :], index_ref, edge_sems.at[3])
    gain_in = pltpu.make_async_copy(gain_hbm, gain_ref, edge_sems.at[4])
    index_in.start()
    gain_in.start()
    cot_in = pltpu.make_async_copy(cot_hbm, cot_ref, edge_sems.at[0])
    stream_in = pltpu.make_async_copy(stream_hbm, stream_ref, edge_sems.at[1])
    cot_in.start()
    stream_in.start()
    index_in.wait()
    index = index_ref[...].astype(F32).T
    pick_ref[...] = one_hot_slots(most, device_ref[0], index, member_ref, *pick_ref.shape)
    stream_in.wait()
    wide = stream_ref[...].astype(F32)
    inv = lax.rsqrt(jnp.mean(wide * wide, axis=1, keepdims=True) + EPS)
    gain_in.wait()
    x_ref[...] = (wide * inv * gain_ref[...]).astype(BF16)
    cot_in.wait()
    copies = send_rows(pick_ref, (x_ref, cot_ref), out_hbm, out_ref, sems)
    x_out = pltpu.make_async_copy(x_ref, x_hbm, edge_sems.at[2])
    x_out.start()
    for part in copies + [x_out]:
        part.wait()


def prepare(most, side, device, index, gain, cotangent, stream):
    tok, width = stream.shape
    experts, cap = index.shape
    experts = experts // 2
    rows = experts * most
    hbm = pl.BlockSpec(memory_space=pl.ANY)
    return pl.pallas_call(
        functools.partial(prepare_kernel, most),
        in_specs=[pl.BlockSpec(memory_space=pltpu.SMEM)] * 2 + [hbm] * 4,
        out_specs=[hbm] * 2,
        scratch_shapes=[pltpu.VMEM((experts, cap), jnp.int32), pltpu.VMEM((1, width), F32)]
        + [pltpu.VMEM((tok, width), BF16)] * 3
        + [
            pltpu.VMEM((rows, 2 * width), BF16),
            pltpu.VMEM((rows, tok), BF16),
            pltpu.VMEM((experts, tok), F32),
            pltpu.SemaphoreType.DMA((width // CHUNK,)),
            pltpu.SemaphoreType.DMA((5,)),
        ],
        out_shape=[jax.ShapeDtypeStruct((tok, width), BF16), jax.ShapeDtypeStruct((rows, 2 * width), BF16)],
        compiler_params=params(),
        cost_estimate=cost(1, 1),
        name="prepare_rows",
    )(side, device, index, gain, cotangent, stream)


def pack(pick, source, which, out=None):
    rows, width = pick.shape[0], source.shape[1]
    step = WIDE

    def kernel(pick_hbm, source_hbm, _, out_hbm, pick_ref, source_ref, out_ref, sems):
        steps = width // step
        pick_in = pltpu.make_async_copy(pick_hbm, pick_ref, sems.at[2 * steps])
        pick_in.start()
        loads = []
        for j in range(0, width, step):
            at = slice(j, j + step)
            loads.append(pltpu.make_async_copy(source_hbm.at[:, at], source_ref.at[:, at], sems.at[steps + len(loads)]))
            loads[-1].start()
        pick_in.wait()
        copies = []
        for j in range(0, width, step):
            at = slice(j, j + step)
            loads[len(copies)].wait()
            out_ref[:, at] = mm(pick_ref[...], source_ref[:, at]).astype(BF16)
            there = out_hbm.at[:, which * width + j : which * width + j + step]
            copies.append(pltpu.make_async_copy(out_ref.at[:, at], there, sems.at[len(copies)]))
            copies[-1].start()
        for part in copies:
            part.wait()

    hbm = pl.BlockSpec(memory_space=pl.ANY)
    return pl.pallas_call(
        kernel,
        in_specs=[hbm] * 3,
        out_specs=hbm,
        out_shape=jax.ShapeDtypeStruct((rows, 2 * width), BF16),
        scratch_shapes=[
            pltpu.VMEM(pick.shape, BF16),
            pltpu.VMEM(source.shape, BF16),
            pltpu.VMEM((rows, width), BF16),
            pltpu.SemaphoreType.DMA((2 * width // step + 1,)),
        ],
        input_output_aliases={} if out is None else {2: 0},
        compiler_params=params(),
        cost_estimate=cost(1, 1),
        name="pack_rows",
    )(pick, source, source if out is None else out)


def streamed(work, name, scalar, ins, outs):
    width = max(x.shape[-1] for x in ins)
    steps = width // WIDE
    group = WIDE // HEAD

    def part(ref, j):
        if len(ref.shape) == 2:
            return ref.at[:, j * WIDE : (j + 1) * WIDE]
        return ref.at[j * group : (j + 1) * group]

    def kernel(*refs):
        scalar_ref, refs = refs[0], refs[1:]
        n, m = len(ins), len(outs)
        in_hbm, out_hbm, in_ref, out_ref = refs[:n], refs[n : n + m], refs[n + m : 2 * n + m], refs[2 * n + m : -1]
        count = iter(range(steps * (n + m)))

        def copy(source, target):
            made = pltpu.make_async_copy(source, target, refs[-1].at[next(count)])
            made.start()
            return made

        def used(ref):
            return [j for j in range(steps) if len(ref.shape) == 2 or j * group < ref.shape[0]]

        loads = [[] for _ in range(steps)]
        for j in range(steps):
            for a, b in zip(in_hbm, in_ref):
                if j in used(a):
                    loads[j].append(copy(part(a, j), part(b, j)))
        stores = []
        for j in range(steps):
            for load in loads[j]:
                load.wait()
            for h in range(j * group, (j + 1) * group):
                work(scalar_ref, h, slice(h * HEAD, (h + 1) * HEAD), in_ref, out_ref)
            stores += [copy(part(a, j), part(b, j)) for a, b in zip(out_ref, out_hbm) if len(a.shape) == 2]
        stores += [copy(a, b) for a, b in zip(out_ref, out_hbm) if len(a.shape) == 3]
        for store in stores:
            store.wait()

    hbm = pl.BlockSpec(memory_space=pl.ANY)
    return pl.pallas_call(
        kernel,
        in_specs=[pl.BlockSpec(memory_space=pltpu.SMEM)] + [hbm] * len(ins),
        out_specs=[hbm] * len(outs),
        out_shape=outs,
        scratch_shapes=[pltpu.VMEM(x.shape, x.dtype) for x in [*ins, *outs]]
        + [pltpu.SemaphoreType.DMA((steps * (len(ins) + len(outs)),))],
        compiler_params=params(),
        cost_estimate=cost(1, 1),
        name=name,
    )(scalar, *ins)


def triangle(tok):
    return lax.broadcasted_iota(jnp.int32, (tok, tok), 0), lax.broadcasted_iota(jnp.int32, (tok, tok), 1)


def early_kernel(
    parity_ref, q_hbm, k_hbm, v_hbm, mine_hbm, other_hbm, mix_hbm, q_ref, k_ref, v_ref, mine_ref, other_ref, mix_ref, sems
):
    pairs = [(k_hbm, k_ref), (v_hbm, v_ref), (q_hbm, q_ref)]
    loads = [pltpu.make_async_copy(a, b, sems.at[i]) for i, (a, b) in enumerate(pairs)]
    for load in loads:
        load.start()
    loads[0].wait()
    loads[1].wait()
    half = mine_ref.shape[0]
    stores = []
    sides = ((other_ref, other_hbm, (1 - parity_ref[0]) * half), (mine_ref, mine_hbm, parity_ref[0] * half))
    for state_ref, state_hbm, first in sides:
        for h in range(half):
            at = pl.ds(pl.multiple_of((first + h) * HEAD, HEAD), HEAD)
            state_ref[h] = mm(k_ref[:, at], v_ref[:, at], TN).astype(BF16)
        stores.append(pltpu.make_async_copy(state_ref, state_hbm, sems.at[3 + len(stores)]))
        stores[-1].start()
    loads[2].wait()
    row, col = triangle(q_ref.shape[0])
    for h in range(2 * half):
        at = slice(h * HEAD, (h + 1) * HEAD)
        mix_ref[:, at] = jnp.where(row <= col, mm(k_ref[:, at], q_ref[:, at], NT), 0.0).astype(BF16)
    stores.append(pltpu.make_async_copy(mix_ref, mix_hbm, sems.at[5]))
    stores[-1].start()
    for store in stores:
        store.wait()


def early(parity, queries, keys, values):
    tok, width = queries.shape
    hbm = pl.BlockSpec(memory_space=pl.ANY)
    shapes = [(width // HEAD // 2, HEAD, HEAD)] * 2 + [(tok, width)]
    return pl.pallas_call(
        early_kernel,
        in_specs=[pl.BlockSpec(memory_space=pltpu.SMEM)] + [hbm] * 3,
        out_specs=[hbm] * 3,
        out_shape=[jax.ShapeDtypeStruct(shape, BF16) for shape in shapes],
        scratch_shapes=[pltpu.VMEM(shape, BF16) for shape in [(tok, width)] * 3 + shapes]
        + [pltpu.SemaphoreType.DMA((6,))],
        compiler_params=params(),
        cost_estimate=cost(1, 1),
        name="early_states",
    )(parity, queries, keys, values)


def combine_kernel(
    parity_ref, pick_hbm, gain_hbm, stream_hbm, back_hbm, cot_hbm, q_hbm, grad_hbm, mine_hbm, other_hbm,
    stream_ref, back_ref, cot_ref, q_ref, grad_ref, normed_ref, sum_ref, pick_ref, gain_ref, mine_ref, other_ref, sems,
):
    width = stream_ref.shape[1]
    count = iter(range(sems.shape[0]))
    pieces = [slice(j, j + WIDE) for j in range(0, width, WIDE)]

    def copy(source, target):
        made = pltpu.make_async_copy(source, target, sems.at[next(count)])
        made.start()
        return made

    stream_in = copy(stream_hbm, stream_ref)
    small_in = [copy(pick_hbm, pick_ref), copy(gain_hbm, gain_ref)]
    back_in = [copy(back_hbm.at[:, at], back_ref.at[:, at]) for at in pieces]
    cot_in = copy(cot_hbm, cot_ref)
    q_in = copy(q_hbm, q_ref)
    stream_in.wait()
    wide = stream_ref[...].astype(F32)
    inv = lax.rsqrt(jnp.mean(wide * wide, axis=1, keepdims=True) + EPS)
    normed_ref[...] = wide * inv
    for part in small_in:
        part.wait()
    total = 0.0
    for part, at in zip(back_in, pieces):
        part.wait()
        grad_normed = mm(pick_ref[...], back_ref[:, at]) * gain_ref[:, at]
        sum_ref[:, at] = grad_normed
        total += jnp.sum(grad_normed * normed_ref[:, at], axis=1, keepdims=True)
    mean = total * (1.0 / width)
    cot_in.wait()
    for at in pieces:
        grad = cot_ref[:, at].astype(F32) + inv * (sum_ref[:, at] - normed_ref[:, at] * mean)
        grad_ref[:, at] = grad.astype(BF16)
    out = [copy(grad_ref, grad_hbm)]
    q_in.wait()
    half = mine_ref.shape[0]
    sides = ((other_ref, other_hbm, (1 - parity_ref[0]) * half), (mine_ref, mine_hbm, parity_ref[0] * half))
    for state_ref, state_hbm, first in sides:
        for h in range(half):
            at = pl.ds(pl.multiple_of((first + h) * HEAD, HEAD), HEAD)
            state_ref[h] = mm(q_ref[:, at], grad_ref[:, at], TN).astype(BF16)
        out += [copy(state_ref, state_hbm)]
    for part in out:
        part.wait()


def combine(parity, pick_t, gain, stream, back, cotangent, queries):
    tok, width = stream.shape
    hbm = pl.BlockSpec(memory_space=pl.ANY)
    return pl.pallas_call(
        combine_kernel,
        in_specs=[pl.BlockSpec(memory_space=pltpu.SMEM)] + [hbm] * 6,
        out_specs=[hbm] * 3,
        out_shape=[jax.ShapeDtypeStruct((tok, width), BF16)]
        + [jax.ShapeDtypeStruct((width // HEAD // 2, HEAD, HEAD), BF16)] * 2,
        scratch_shapes=[pltpu.VMEM((tok, width), BF16), pltpu.VMEM(back.shape, BF16)]
        + [pltpu.VMEM((tok, width), BF16)] * 3
        + [pltpu.VMEM((tok, width), F32)] * 2
        + [pltpu.VMEM(pick_t.shape, BF16), pltpu.VMEM((1, width), F32)]
        + [pltpu.VMEM((width // HEAD // 2, HEAD, HEAD), BF16)] * 2
        + [pltpu.SemaphoreType.DMA((width // WIDE + 8,))],
        compiler_params=params(),
        cost_estimate=cost(2 * tok * width * (back.shape[0] + HEAD), 2 * width * (back.shape[0] + 6 * tok)),
        name="combine_rows",
    )(parity, pick_t, gain, stream, back, cotangent, queries)


def expert_kernel(
    first_ref, gates_hbm, in_hbm, wg_hbm, wu_hbm, wd_hbm, _,
    back_hbm, ggp_hbm, gup_hbm, hid_hbm, router_hbm, gain_hbm,
    in_ref, wg_ref, wu_ref, wd_ref, back_ref, ggp_ref, gup_ref, hid_ref, gates_ref, router_ref, gain_ref, sems,
):
    width = wg_ref.shape[0]
    slots = in_ref.shape[0]
    count = iter(range(sems.shape[0]))
    pieces = [slice(j, j + CHUNK) for j in range(0, width, CHUNK)]
    shifted = [slice(j, j + CHUNK) for j in range(width, 2 * width, CHUNK)]

    def copy(source, target):
        made = pltpu.make_async_copy(source, target, sems.at[next(count)])
        made.start()
        return made

    loads = []
    for at in pieces:
        loads += [copy(in_hbm.at[:, at], in_ref.at[:, at]), copy(wg_hbm.at[at, :], wg_ref.at[at, :])]
        loads += [copy(wu_hbm.at[at, :], wu_ref.at[at, :])]
    for at, there in zip(pieces, shifted):
        loads += [copy(in_hbm.at[:, there], in_ref.at[:, there]), copy(wd_hbm.at[:, at], wd_ref.at[:, at])]
    gates_in = copy(gates_hbm, gates_ref)
    loads = iter(loads)
    gate_pre = up_pre = raw_hidden = 0.0
    for at in pieces:
        for _ in range(3):
            next(loads).wait()
        gate_pre += mm(in_ref[:, at], wg_ref[at, :])
        up_pre += mm(in_ref[:, at], wu_ref[at, :])
    for at, there in zip(pieces, shifted):
        for _ in range(2):
            next(loads).wait()
        raw_hidden += mm(in_ref[:, there], wd_ref[:, at], NT)
    same = lax.broadcasted_iota(jnp.int32, (slots, slots), 0) == lax.broadcasted_iota(jnp.int32, (slots, slots), 1)
    gates_in.wait()
    gates = jnp.sum(jnp.where(same, gates_ref[...], 0.0), axis=1, keepdims=True)
    sigmoid = 1.0 / (1.0 + jnp.exp(-gate_pre))
    silu = gate_pre * sigmoid
    hidden = silu * up_pre
    grad_hidden = gates * raw_hidden
    slope = sigmoid * (1.0 + gate_pre * (1.0 - sigmoid))
    ggp_ref[...] = (grad_hidden * up_pre * slope).astype(BF16)
    gup_ref[...] = (grad_hidden * silu).astype(BF16)
    out = [copy(ggp_ref, ggp_hbm), copy(gup_ref, gup_hbm)]
    hid_ref[...] = (hidden * gates).astype(BF16)
    router = jnp.sum(hidden.astype(BF16).astype(F32) * raw_hidden, axis=1, keepdims=True)
    router_ref[...] = jnp.sum(jnp.where(same, router, 0.0), axis=0, keepdims=True)
    out += [copy(hid_ref, hid_hbm), copy(router_ref, router_hbm)]
    first = pl.ds(pl.multiple_of(first_ref[0] * slots, slots), slots)
    for at in pieces:
        grad = mm(ggp_ref[...], wg_ref[at, :], NT) + mm(gup_ref[...], wu_ref[at, :], NT)
        back_ref[:, at] = grad.astype(BF16)
        out += [copy(back_ref.at[:, at], back_hbm.at[first, at])]
        gain_ref[:, at] = jnp.sum(back_ref[:, at].astype(F32) * in_ref[:, at].astype(F32), axis=0, keepdims=True)
    out += [copy(gain_ref, gain_hbm)]
    for part in out:
        part.wait()


def expert(first, gates, incoming, w_gate, w_up, w_down, back=None):
    slots = incoming.shape[0]
    width, inner = w_gate.shape
    hbm = pl.BlockSpec(memory_space=pl.ANY)
    small = [(slots, inner)] * 3
    held = [incoming.shape, w_gate.shape, w_up.shape, w_down.shape, (slots, width)] + small
    alias = {} if back is None else {6: 0}
    if back is None:
        back = gates
    return pl.pallas_call(
        expert_kernel,
        in_specs=[pl.BlockSpec(memory_space=pltpu.SMEM)] + [hbm] * 6,
        out_specs=[hbm] * 6,
        out_shape=[jax.ShapeDtypeStruct(shape, BF16) for shape in [(2 * slots, width)] + small]
        + [jax.ShapeDtypeStruct((1, slots), F32), jax.ShapeDtypeStruct((1, width), F32)],
        scratch_shapes=[pltpu.VMEM(shape, BF16) for shape in held]
        + [pltpu.VMEM((1, size), F32) for size in (slots, slots, width)]
        + [pltpu.SemaphoreType.DMA((6 * width // CHUNK + 6,))],
        input_output_aliases=alias,
        compiler_params=params(),
        cost_estimate=cost(10 * slots * width * inner, 6 * width * (inner + slots)),
        name="expert_rows",
    )(first, gates, incoming, w_gate, w_up, w_down, back)


def add_across(value, bit):
    count = lax.axis_size("grp") * lax.axis_size("seq")
    return value + lax.ppermute(value, AXES, [(i, i ^ bit) for i in range(count)])


def query_part(scale, parity, keys, values, grad, prior):
    tok, width = keys.shape

    def work(_, h, at, ins, outs):
        k_ref, v_ref, g_ref, prior_ref = ins
        row, col = triangle(tok)
        g = g_ref[:, at]
        mix_a = jnp.where(row >= col, mm(g, v_ref[:, at], NT), 0.0).astype(BF16)
        outs[0][:, at] = (scale * (mm(mix_a, k_ref[:, at]) + mm(g, prior_ref[h], NT))).astype(BF16)

    outs = [jax.ShapeDtypeStruct((tok, width), BF16)]
    return streamed(work, "query_attention", parity, [keys, values, grad, prior], outs)


def local_part(parity, queries, values, grad, mix):
    tok, width = queries.shape

    def work(_, h, at, ins, outs):
        q_ref, v_ref, g_ref, mix_ref = ins
        row, col = triangle(tok)
        g = g_ref[:, at]
        mix_t = jnp.where(row <= col, mm(v_ref[:, at], g, NT), 0.0).astype(BF16)
        outs[0][:, at] = mm(mix_t, q_ref[:, at]).astype(BF16)
        outs[1][:, at] = mm(mix_ref[:, at], g).astype(BF16)

    outs = [jax.ShapeDtypeStruct((tok, width), BF16)] * 2
    return streamed(work, "local_attention", parity, [queries, values, grad, mix], outs)


def last_part(scale, parity, keys, values, pk, pv, own, other):
    tok, width = keys.shape
    half = own.shape[0]

    def work(parity_ref, h, at, ins, outs):
        k_ref, v_ref, pk_ref, pv_ref, own_ref, other_ref = ins
        gk_ref, gv_ref = outs
        later = jnp.where(parity_ref[0] == h // half, own_ref[h % half], other_ref[h % half])
        gk_ref[:, at] = (scale * (pk_ref[:, at].astype(F32) + mm(v_ref[:, at], later, NT))).astype(BF16)
        gv_ref[:, at] = (scale * (pv_ref[:, at].astype(F32) + mm(k_ref[:, at], later))).astype(BF16)

    outs = [jax.ShapeDtypeStruct((tok, width), BF16)] * 2
    return streamed(work, "last_attention", parity, [keys, values, pk, pv, own, other], outs)


def states_beyond(place, mine, other, beside):
    count = lax.axis_size("seq")
    parity = place & 1

    def swap(value, bit):
        return lax.ppermute(value.astype(BF16), "seq", [(i, i ^ bit) for i in range(count)])

    bits = [1 << b for b in range(1, count.bit_length() - 1)]
    quarter = mine.shape[0] // 2
    partner = swap(other, 1).astype(F32)
    mine = mine.astype(F32)
    both = mine + partner
    rising_sum, falling_base = both[:quarter], both[quarter:]
    rising = jnp.zeros_like(rising_sum)
    falling = jnp.zeros_like(falling_base)
    beside_out = []
    for up, down in zip(bits, reversed(bits)):
        got_up = swap(rising_sum, up)
        got_down = swap(falling + jnp.where((place & down) == 0, 0.0, falling_base), down)
        if beside:
            got_up, got_down, done = lax.optimization_barrier((got_up, got_down, beside.pop(0)(rising_sum)))
            beside_out.append(done)
        got_up, got_down = got_up.astype(F32), got_down.astype(F32)
        rising = rising + jnp.where((place & up) == 0, got_up, 0.0)
        rising_sum = rising_sum + got_up
        falling = falling + got_down
    own = jnp.concatenate([rising, falling])
    theirs = swap(own + jnp.where(parity == 1, mine, 0.0), 1)
    own = (own + jnp.where(parity == 0, partner, 0.0)).astype(BF16)
    return own, theirs, beside_out + [work(rising_sum) for work in beside]


def body(
    stream,
    cotangent,
    norm_gain,
    queries,
    key_vectors,
    value_vectors,
    expert_index,
    router_gates,
    gate_proj,
    up_proj,
    down_proj,
):
    tok, width = stream.shape
    seq_count = lax.axis_size("seq")
    dev_count = seq_count * lax.axis_size("grp")
    experts, capacity = expert_index.shape
    most = 2 * capacity // dev_count
    here = lax.axis_index("grp") * seq_count + lax.axis_index("seq")
    scale = 1.0 / math.sqrt(HEAD * tok * seq_count)
    gain = norm_gain[None, :]
    w_gate, w_up, w_down = gate_proj[0], up_proj[0], down_proj[0]

    halves = dev_count // 2
    swap = [(i, (i + halves) % dev_count) for i in range(dev_count)]
    groups = [[side * halves + i for i in range(halves)] for side in range(2)]
    side = here // halves
    side_array = side.astype(jnp.int32)[None]
    parity = (lax.axis_index("seq") & 1).astype(jnp.int32)[None]
    here_array = here.astype(jnp.int32)[None]
    there_array = ((here + halves) % dev_count).astype(jnp.int32)[None]

    def exchange(value):
        return lax.all_to_all(value, AXES, split_axis=0, concat_axis=0, tiled=True, axis_index_groups=groups)

    inputs, out_own = prepare(most, side_array, here_array, expert_index, gain, cotangent, stream)
    own = exchange(out_own)
    far_cot = lax.ppermute(cotangent, AXES, swap)
    far_inputs = lax.ppermute(inputs, AXES, swap)

    pick_t = picks(most, tok, here_array, expert_index).T
    half_index = lax.dynamic_slice_in_dim(expert_index, side * (experts // 2), experts // 2, 0)
    far_pick = picks(most, tok, there_array, half_index)
    own_index = lax.dynamic_index_in_dim(expert_index, here, 0, keepdims=False)
    source = own_index // tok
    ahead = (source[None, :] == source[:, None]) & (own_index[None, :] < own_index[:, None])
    before = jnp.sum(ahead.astype(jnp.int32), axis=1)
    arrival = jnp.where(source // halves == side, source % halves, halves + source % halves) * most + before
    place_t = arrival[None, :] == jnp.arange(dev_count * most)[:, None]
    slot_gates = jnp.sum(jnp.where(place_t, router_gates, 0.0), axis=1).reshape(2, 1, halves * most)
    far_out = pack(far_pick, far_cot, 1)
    far_inputs, far_out, pick_t, slot_gates = lax.optimization_barrier((far_inputs, far_out, pick_t, slot_gates))
    far_out = pack(far_pick, far_inputs, 0, far_out)
    far = exchange(far_out)

    own, far_out, q_early, k_early, v_early = lax.optimization_barrier(
        (own, far_out, queries, key_vectors, value_vectors)
    )
    key_mine, key_other, mix_b = early(parity, q_early, k_early, v_early)
    back, own_ggp, own_gup, own_hidden, own_router, own_gain = expert(
        side_array, slot_gates[0], own, w_gate, w_up, w_down
    )
    far, back, key_mine, key_other, mix_b = lax.optimization_barrier((far, back, key_mine, key_other, mix_b))
    back, far_ggp, far_gup, far_hidden, far_router, far_gain = expert(
        1 - side_array, slot_gates[1], far, w_gate, w_up, w_down, back
    )
    returned = lax.all_to_all(back, AXES, split_axis=0, concat_axis=0, tiled=True)

    place = lax.axis_index("seq")
    own_prior, other_prior, _ = states_beyond(seq_count - 1 - place, key_mine, key_other, [])
    is_low = parity[0] == 0
    prior = jnp.concatenate(
        [jnp.where(is_low, own_prior, other_prior), jnp.where(is_low, other_prior, own_prior)]
    )
    own, far, far_ggp, back = lax.optimization_barrier((own, far, far_ggp, back))
    arrived = jnp.concatenate([own, far])
    arrived, own_gain, far_gain = lax.optimization_barrier((arrived, own_gain, far_gain))
    gain_total = (own_gain + far_gain) / gain
    bits = [1 << b for b in range(dev_count.bit_length() - 1)]
    for bit in bits[:-2]:
        gain_total = add_across(gain_total, bit)
    rows, dy_rows = arrived[:, :width], arrived[:, width:]
    grad_gate_pre = jnp.concatenate([own_ggp, far_ggp])
    grad_up_pre = jnp.concatenate([own_gup, far_gup])
    hidden = jnp.concatenate([own_hidden, far_hidden])
    grad_gate = lax.dot_general(rows, grad_gate_pre, TN, preferred_element_type=F32).astype(BF16)
    grad_up = lax.dot_general(rows, grad_up_pre, TN, preferred_element_type=F32).astype(BF16)
    grad_down = lax.dot_general(hidden, dy_rows, TN, preferred_element_type=F32).astype(BF16)
    slot_router = jnp.concatenate([own_router, far_router], axis=1).reshape(dev_count * most, 1)
    router = jnp.sum(jnp.where(place_t, slot_router, 0.0), axis=0, keepdims=True)
    returned, grad_gate, grad_up, grad_down, router, gain_total, prior, mix_b = lax.optimization_barrier(
        (returned, grad_gate, grad_up, grad_down, router, gain_total, prior, mix_b)
    )

    grad_stream, mine, other = combine(parity, pick_t, gain, stream, returned, cotangent, queries)

    gain_across = [(i, i ^ bits[-1]) for i in range(dev_count)]
    gain_sums = [gain_total]

    def first(_):
        gain_sums.append(add_across(gain_total, bits[-2]))
        return local_part(parity, queries, value_vectors, grad_stream, mix_b), gain_sums[-1]

    def second(after):
        grad, _ = lax.optimization_barrier((grad_stream, after))
        done = query_part(scale, parity, key_vectors, value_vectors, grad, prior)
        return done, lax.ppermute(gain_sums[-1], AXES, gain_across)

    own_state, other_state, done = states_beyond(place, mine, other, [first, second])
    ((part_k, part_v), gain_total), ((grad_queries,), gain_other) = done
    gain_total += gain_other
    grad_keys, grad_values = last_part(
        scale, parity, key_vectors, value_vectors, part_k, part_v, own_state, other_state
    )
    return (
        grad_stream,
        grad_queries,
        grad_keys,
        grad_values,
        grad_gate[None],
        grad_up[None],
        grad_down[None],
        router,
        gain_total[0],
    )


def solution(mesh):
    rows = P(AXES, None)
    cube = P(AXES, None, None)
    in_specs = (rows, rows, P(), rows, rows, rows, P(), rows, cube, cube, cube)
    out_specs = (rows, rows, rows, rows, cube, cube, cube, rows, P())
    return jax.shard_map(body, mesh=mesh, in_specs=in_specs, out_specs=out_specs, check_vma=False)
```

```python
import functools
import math

import jax
import jax.numpy as jnp
from jax import lax
from jax.experimental import pallas as pl
from jax.experimental.pallas import tpu as pltpu
from jax.sharding import PartitionSpec as P

HEAD = 128
EPS = 1e-06
F32 = jnp.float32
BF16 = jnp.bfloat16
AXES = ("grp", "seq")
VMEM_LIMIT = 63 * 1024 * 1024
CHUNK = 512
WIDE = 1024

NN = (((1,), (0,)), ((), ()))
NT = (((1,), (1,)), ((), ()))
TN = (((0,), (0,)), ((), ()))


def mm(a, b, dims=NN):
    return lax.dot_general(a, b, dims, preferred_element_type=F32)


def params():
    return pltpu.CompilerParams(vmem_limit_bytes=VMEM_LIMIT)


def cost(flops, moved):
    return pl.CostEstimate(flops=flops, bytes_accessed=moved, transcendentals=0)


def one_hot_slots(most, device, index, member_ref, rows, tok):
    cap, experts = index.shape
    token = (lax.broadcasted_iota(jnp.int32, (cap, tok), 1) + device * tok).astype(F32)
    for e in range(experts):
        same = index[:, e : e + 1] == token
        member_ref[e : e + 1, :] = jnp.sum(same.astype(F32), axis=0, keepdims=True)
    member = member_ref[...]
    before = lax.broadcasted_iota(jnp.int32, (tok, tok), 0) < lax.broadcasted_iota(jnp.int32, (tok, tok), 1)
    rank = mm(member.astype(BF16), before.astype(BF16))
    value = jnp.where(member > 0.0, rank, -1.0).astype(BF16)
    row = lax.broadcasted_iota(jnp.int32, (rows, experts), 0)
    first = lax.broadcasted_iota(jnp.int32, (rows, experts), 1) * most
    owner = (row >= first) & (row < first + most)
    spread = mm(owner.astype(BF16), value)
    place = jnp.sum(jnp.where(owner, row - first, 0), axis=1, keepdims=True)
    return (spread == place.astype(F32)).astype(BF16)


def pick_kernel(most, device_ref, index_ref, pick_ref, member_ref):
    index = index_ref[...].astype(F32).T
    pick_ref[...] = one_hot_slots(most, device_ref[0], index, member_ref, *pick_ref.shape)


def picks(most, tok, device, index):
    experts, cap = index.shape
    return pl.pallas_call(
        functools.partial(pick_kernel, most),
        in_specs=[pl.BlockSpec(memory_space=pltpu.SMEM), pl.BlockSpec(memory_space=pltpu.VMEM)],
        out_specs=pl.BlockSpec(memory_space=pltpu.VMEM),
        out_shape=jax.ShapeDtypeStruct((experts * most, tok), BF16),
        scratch_shapes=[pltpu.VMEM((experts, tok), F32)],
        compiler_params=params(),
        cost_estimate=cost(1, 1),
        name="pick_slots",
    )(device, index)


def send_rows(pick_ref, source, first, out_hbm, out_ref, sems):
    copies = []
    width = source.shape[1]
    for j in range(0, width, WIDE):
        at = slice(first + j, first + j + WIDE)
        out_ref[:, at] = mm(pick_ref[...], source[:, j : j + WIDE]).astype(BF16)
        copies.append(pltpu.make_async_copy(out_ref.at[:, at], out_hbm.at[:, at], sems.at[(first + j) // WIDE]))
        copies[-1].start()
    return copies


def prepare_kernel(
    most, half_ref, device_ref, index_hbm, gain_hbm, cot_hbm, stream_hbm, x_hbm, out_hbm,
    index_ref, gain_ref, cot_ref, stream_ref, x_ref, out_ref, pick_ref, member_ref, sems, edge_sems,
):
    half = index_ref.shape[0]
    first = pl.ds(pl.multiple_of(half_ref[0] * half, half), half)
    index_in = pltpu.make_async_copy(index_hbm.at[first, :], index_ref, edge_sems.at[3])
    gain_in = pltpu.make_async_copy(gain_hbm, gain_ref, edge_sems.at[4])
    index_in.start()
    gain_in.start()
    cot_in = pltpu.make_async_copy(cot_hbm, cot_ref, edge_sems.at[0])
    stream_in = pltpu.make_async_copy(stream_hbm, stream_ref, edge_sems.at[1])
    cot_in.start()
    stream_in.start()
    index_in.wait()
    index = index_ref[...].astype(F32).T
    pick_ref[...] = one_hot_slots(most, device_ref[0], index, member_ref, *pick_ref.shape)
    cot_in.wait()
    copies = send_rows(pick_ref, cot_ref, cot_ref.shape[1], out_hbm, out_ref, sems)
    stream_in.wait()
    wide = stream_ref[...].astype(F32)
    inv = lax.rsqrt(jnp.mean(wide * wide, axis=1, keepdims=True) + EPS)
    gain_in.wait()
    x_ref[...] = (wide * inv * gain_ref[...]).astype(BF16)
    x_out = pltpu.make_async_copy(x_ref, x_hbm, edge_sems.at[2])
    x_out.start()
    copies += send_rows(pick_ref, x_ref, 0, out_hbm, out_ref, sems)
    for part in copies + [x_out]:
        part.wait()


def prepare(most, side, device, index, gain, cotangent, stream):
    tok, width = stream.shape
    experts, cap = index.shape
    experts = experts // 2
    rows = experts * most
    hbm = pl.BlockSpec(memory_space=pl.ANY)
    return pl.pallas_call(
        functools.partial(prepare_kernel, most),
        in_specs=[pl.BlockSpec(memory_space=pltpu.SMEM)] * 2 + [hbm] * 4,
        out_specs=[hbm] * 2,
        scratch_shapes=[pltpu.VMEM((experts, cap), jnp.int32), pltpu.VMEM((1, width), F32)]
        + [pltpu.VMEM((tok, width), BF16)] * 3
        + [
            pltpu.VMEM((rows, 2 * width), BF16),
            pltpu.VMEM((rows, tok), BF16),
            pltpu.VMEM((experts, tok), F32),
            pltpu.SemaphoreType.DMA((width // CHUNK,)),
            pltpu.SemaphoreType.DMA((5,)),
        ],
        out_shape=[jax.ShapeDtypeStruct((tok, width), BF16), jax.ShapeDtypeStruct((rows, 2 * width), BF16)],
        compiler_params=params(),
        cost_estimate=cost(1, 1),
        name="prepare_rows",
    )(side, device, index, gain, cotangent, stream)


def pack(pick, source, which, out=None):
    rows, width = pick.shape[0], source.shape[1]
    step = WIDE

    def kernel(pick_hbm, source_hbm, _, out_hbm, pick_ref, source_ref, out_ref, sems):
        steps = width // step
        pick_in = pltpu.make_async_copy(pick_hbm, pick_ref, sems.at[2 * steps])
        pick_in.start()
        loads = []
        for j in range(0, width, step):
            at = slice(j, j + step)
            loads.append(pltpu.make_async_copy(source_hbm.at[:, at], source_ref.at[:, at], sems.at[steps + len(loads)]))
            loads[-1].start()
        pick_in.wait()
        copies = []
        for j in range(0, width, step):
            at = slice(j, j + step)
            loads[len(copies)].wait()
            out_ref[:, at] = mm(pick_ref[...], source_ref[:, at]).astype(BF16)
            there = out_hbm.at[:, which * width + j : which * width + j + step]
            copies.append(pltpu.make_async_copy(out_ref.at[:, at], there, sems.at[len(copies)]))
            copies[-1].start()
        for part in copies:
            part.wait()

    hbm = pl.BlockSpec(memory_space=pl.ANY)
    return pl.pallas_call(
        kernel,
        in_specs=[hbm] * 3,
        out_specs=hbm,
        out_shape=jax.ShapeDtypeStruct((rows, 2 * width), BF16),
        scratch_shapes=[
            pltpu.VMEM(pick.shape, BF16),
            pltpu.VMEM(source.shape, BF16),
            pltpu.VMEM((rows, width), BF16),
            pltpu.SemaphoreType.DMA((2 * width // step + 1,)),
        ],
        input_output_aliases={} if out is None else {2: 0},
        compiler_params=params(),
        cost_estimate=cost(1, 1),
        name="pack_rows",
    )(pick, source, source if out is None else out)


def streamed(work, name, scalar, ins, outs):
    width = max(x.shape[-1] for x in ins)
    steps = width // WIDE
    group = WIDE // HEAD

    def part(ref, j):
        if len(ref.shape) == 2:
            return ref.at[:, j * WIDE : (j + 1) * WIDE]
        return ref.at[j * group : (j + 1) * group]

    def kernel(*refs):
        scalar_ref, refs = refs[0], refs[1:]
        n, m = len(ins), len(outs)
        in_hbm, out_hbm, in_ref, out_ref = refs[:n], refs[n : n + m], refs[n + m : 2 * n + m], refs[2 * n + m : -1]
        count = iter(range(steps * (n + m)))

        def copy(source, target):
            made = pltpu.make_async_copy(source, target, refs[-1].at[next(count)])
            made.start()
            return made

        def used(ref):
            return [j for j in range(steps) if len(ref.shape) == 2 or j * group < ref.shape[0]]

        loads = [[] for _ in range(steps)]
        for j in range(steps):
            for a, b in zip(in_hbm, in_ref):
                if j in used(a):
                    loads[j].append(copy(part(a, j), part(b, j)))
        stores = []
        for j in range(steps):
            for load in loads[j]:
                load.wait()
            for h in range(j * group, (j + 1) * group):
                work(scalar_ref, h, slice(h * HEAD, (h + 1) * HEAD), in_ref, out_ref)
            stores += [copy(part(a, j), part(b, j)) for a, b in zip(out_ref, out_hbm) if len(a.shape) == 2]
        stores += [copy(a, b) for a, b in zip(out_ref, out_hbm) if len(a.shape) == 3]
        for store in stores:
            store.wait()

    hbm = pl.BlockSpec(memory_space=pl.ANY)
    return pl.pallas_call(
        kernel,
        in_specs=[pl.BlockSpec(memory_space=pltpu.SMEM)] + [hbm] * len(ins),
        out_specs=[hbm] * len(outs),
        out_shape=outs,
        scratch_shapes=[pltpu.VMEM(x.shape, x.dtype) for x in [*ins, *outs]]
        + [pltpu.SemaphoreType.DMA((steps * (len(ins) + len(outs)),))],
        compiler_params=params(),
        cost_estimate=cost(1, 1),
        name=name,
    )(scalar, *ins)


def triangle(tok):
    return lax.broadcasted_iota(jnp.int32, (tok, tok), 0), lax.broadcasted_iota(jnp.int32, (tok, tok), 1)


def early_kernel(
    parity_ref, q_hbm, k_hbm, v_hbm, mine_hbm, other_hbm, mix_hbm, q_ref, k_ref, v_ref, mine_ref, other_ref, mix_ref, sems
):
    pairs = [(k_hbm, k_ref), (v_hbm, v_ref), (q_hbm, q_ref)]
    loads = [pltpu.make_async_copy(a, b, sems.at[i]) for i, (a, b) in enumerate(pairs)]
    for load in loads:
        load.start()
    loads[0].wait()
    loads[1].wait()
    half = mine_ref.shape[0]
    stores = []
    sides = ((other_ref, other_hbm, (1 - parity_ref[0]) * half), (mine_ref, mine_hbm, parity_ref[0] * half))
    for state_ref, state_hbm, first in sides:
        for h in range(half):
            at = pl.ds(pl.multiple_of((first + h) * HEAD, HEAD), HEAD)
            state_ref[h] = mm(k_ref[:, at], v_ref[:, at], TN).astype(BF16)
        stores.append(pltpu.make_async_copy(state_ref, state_hbm, sems.at[3 + len(stores)]))
        stores[-1].start()
    loads[2].wait()
    row, col = triangle(q_ref.shape[0])
    for h in range(2 * half):
        at = slice(h * HEAD, (h + 1) * HEAD)
        mix_ref[:, at] = jnp.where(row <= col, mm(k_ref[:, at], q_ref[:, at], NT), 0.0).astype(BF16)
    stores.append(pltpu.make_async_copy(mix_ref, mix_hbm, sems.at[5]))
    stores[-1].start()
    for store in stores:
        store.wait()


def early(parity, queries, keys, values):
    tok, width = queries.shape
    hbm = pl.BlockSpec(memory_space=pl.ANY)
    shapes = [(width // HEAD // 2, HEAD, HEAD)] * 2 + [(tok, width)]
    return pl.pallas_call(
        early_kernel,
        in_specs=[pl.BlockSpec(memory_space=pltpu.SMEM)] + [hbm] * 3,
        out_specs=[hbm] * 3,
        out_shape=[jax.ShapeDtypeStruct(shape, BF16) for shape in shapes],
        scratch_shapes=[pltpu.VMEM(shape, BF16) for shape in [(tok, width)] * 3 + shapes]
        + [pltpu.SemaphoreType.DMA((6,))],
        compiler_params=params(),
        cost_estimate=cost(1, 1),
        name="early_states",
    )(parity, queries, keys, values)


def combine_kernel(
    parity_ref, pick_hbm, gain_hbm, stream_hbm, back_hbm, cot_hbm, q_hbm, grad_hbm, mine_hbm, other_hbm,
    stream_ref, back_ref, cot_ref, q_ref, grad_ref, normed_ref, sum_ref, pick_ref, gain_ref, mine_ref, other_ref, sems,
):
    width = stream_ref.shape[1]
    count = iter(range(sems.shape[0]))
    pieces = [slice(j, j + WIDE) for j in range(0, width, WIDE)]

    def copy(source, target):
        made = pltpu.make_async_copy(source, target, sems.at[next(count)])
        made.start()
        return made

    stream_in = copy(stream_hbm, stream_ref)
    small_in = [copy(pick_hbm, pick_ref), copy(gain_hbm, gain_ref)]
    back_in = [copy(back_hbm.at[:, at], back_ref.at[:, at]) for at in pieces]
    cot_in = copy(cot_hbm, cot_ref)
    q_in = copy(q_hbm, q_ref)
    stream_in.wait()
    wide = stream_ref[...].astype(F32)
    inv = lax.rsqrt(jnp.mean(wide * wide, axis=1, keepdims=True) + EPS)
    normed_ref[...] = wide * inv
    for part in small_in:
        part.wait()
    total = 0.0
    for part, at in zip(back_in, pieces):
        part.wait()
        grad_normed = mm(pick_ref[...], back_ref[:, at]) * gain_ref[:, at]
        sum_ref[:, at] = grad_normed
        total += jnp.sum(grad_normed * normed_ref[:, at], axis=1, keepdims=True)
    mean = total * (1.0 / width)
    cot_in.wait()
    for at in pieces:
        grad = cot_ref[:, at].astype(F32) + inv * (sum_ref[:, at] - normed_ref[:, at] * mean)
        grad_ref[:, at] = grad.astype(BF16)
    out = [copy(grad_ref, grad_hbm)]
    q_in.wait()
    half = mine_ref.shape[0]
    sides = ((other_ref, other_hbm, (1 - parity_ref[0]) * half), (mine_ref, mine_hbm, parity_ref[0] * half))
    for state_ref, state_hbm, first in sides:
        for h in range(half):
            at = pl.ds(pl.multiple_of((first + h) * HEAD, HEAD), HEAD)
            state_ref[h] = mm(q_ref[:, at], grad_ref[:, at], TN).astype(BF16)
        out += [copy(state_ref, state_hbm)]
    for part in out:
        part.wait()


def combine(parity, pick_t, gain, stream, back, cotangent, queries):
    tok, width = stream.shape
    hbm = pl.BlockSpec(memory_space=pl.ANY)
    return pl.pallas_call(
        combine_kernel,
        in_specs=[pl.BlockSpec(memory_space=pltpu.SMEM)] + [hbm] * 6,
        out_specs=[hbm] * 3,
        out_shape=[jax.ShapeDtypeStruct((tok, width), BF16)]
        + [jax.ShapeDtypeStruct((width // HEAD // 2, HEAD, HEAD), BF16)] * 2,
        scratch_shapes=[pltpu.VMEM((tok, width), BF16), pltpu.VMEM(back.shape, BF16)]
        + [pltpu.VMEM((tok, width), BF16)] * 3
        + [pltpu.VMEM((tok, width), F32)] * 2
        + [pltpu.VMEM(pick_t.shape, BF16), pltpu.VMEM((1, width), F32)]
        + [pltpu.VMEM((width // HEAD // 2, HEAD, HEAD), BF16)] * 2
        + [pltpu.SemaphoreType.DMA((width // WIDE + 8,))],
        compiler_params=params(),
        cost_estimate=cost(2 * tok * width * (back.shape[0] + HEAD), 2 * width * (back.shape[0] + 6 * tok)),
        name="combine_rows",
    )(parity, pick_t, gain, stream, back, cotangent, queries)


def expert_kernel(
    first_ref, gates_hbm, in_hbm, wg_hbm, wu_hbm, wd_hbm, _,
    back_hbm, ggp_hbm, gup_hbm, hid_hbm, router_hbm, gain_hbm,
    in_ref, wg_ref, wu_ref, wd_ref, back_ref, ggp_ref, gup_ref, hid_ref, gates_ref, router_ref, gain_ref, sems,
):
    width = wg_ref.shape[0]
    slots = in_ref.shape[0]
    count = iter(range(sems.shape[0]))
    pieces = [slice(j, j + CHUNK) for j in range(0, width, CHUNK)]
    shifted = [slice(j, j + CHUNK) for j in range(width, 2 * width, CHUNK)]

    def copy(source, target):
        made = pltpu.make_async_copy(source, target, sems.at[next(count)])
        made.start()
        return made

    loads = []
    for at in pieces:
        loads += [copy(in_hbm.at[:, at], in_ref.at[:, at]), copy(wg_hbm.at[at, :], wg_ref.at[at, :])]
        loads += [copy(wu_hbm.at[at, :], wu_ref.at[at, :])]
    for at, there in zip(pieces, shifted):
        loads += [copy(in_hbm.at[:, there], in_ref.at[:, there]), copy(wd_hbm.at[:, at], wd_ref.at[:, at])]
    gates_in = copy(gates_hbm, gates_ref)
    loads = iter(loads)
    gate_pre = up_pre = raw_hidden = 0.0
    for at in pieces:
        for _ in range(3):
            next(loads).wait()
        gate_pre += mm(in_ref[:, at], wg_ref[at, :])
        up_pre += mm(in_ref[:, at], wu_ref[at, :])
    for at, there in zip(pieces, shifted):
        for _ in range(2):
            next(loads).wait()
        raw_hidden += mm(in_ref[:, there], wd_ref[:, at], NT)
    same = lax.broadcasted_iota(jnp.int32, (slots, slots), 0) == lax.broadcasted_iota(jnp.int32, (slots, slots), 1)
    gates_in.wait()
    gates = jnp.sum(jnp.where(same, gates_ref[...], 0.0), axis=1, keepdims=True)
    sigmoid = 1.0 / (1.0 + jnp.exp(-gate_pre))
    silu = gate_pre * sigmoid
    hidden = silu * up_pre
    grad_hidden = gates * raw_hidden
    slope = sigmoid * (1.0 + gate_pre * (1.0 - sigmoid))
    ggp_ref[...] = (grad_hidden * up_pre * slope).astype(BF16)
    gup_ref[...] = (grad_hidden * silu).astype(BF16)
    out = [copy(ggp_ref, ggp_hbm), copy(gup_ref, gup_hbm)]
    hid_ref[...] = (hidden * gates).astype(BF16)
    router = jnp.sum(hidden.astype(BF16).astype(F32) * raw_hidden, axis=1, keepdims=True)
    router_ref[...] = jnp.sum(jnp.where(same, router, 0.0), axis=0, keepdims=True)
    out += [copy(hid_ref, hid_hbm), copy(router_ref, router_hbm)]
    first = pl.ds(pl.multiple_of(first_ref[0] * slots, slots), slots)
    for at in pieces:
        grad = mm(ggp_ref[...], wg_ref[at, :], NT) + mm(gup_ref[...], wu_ref[at, :], NT)
        back_ref[:, at] = grad.astype(BF16)
        out += [copy(back_ref.at[:, at], back_hbm.at[first, at])]
        gain_ref[:, at] = jnp.sum(back_ref[:, at].astype(F32) * in_ref[:, at].astype(F32), axis=0, keepdims=True)
    out += [copy(gain_ref, gain_hbm)]
    for part in out:
        part.wait()


def expert(first, gates, incoming, w_gate, w_up, w_down, back=None):
    slots = incoming.shape[0]
    width, inner = w_gate.shape
    hbm = pl.BlockSpec(memory_space=pl.ANY)
    small = [(slots, inner)] * 3
    held = [incoming.shape, w_gate.shape, w_up.shape, w_down.shape, (slots, width)] + small
    alias = {} if back is None else {6: 0}
    if back is None:
        back = gates
    return pl.pallas_call(
        expert_kernel,
        in_specs=[pl.BlockSpec(memory_space=pltpu.SMEM)] + [hbm] * 6,
        out_specs=[hbm] * 6,
        out_shape=[jax.ShapeDtypeStruct(shape, BF16) for shape in [(2 * slots, width)] + small]
        + [jax.ShapeDtypeStruct((1, slots), F32), jax.ShapeDtypeStruct((1, width), F32)],
        scratch_shapes=[pltpu.VMEM(shape, BF16) for shape in held]
        + [pltpu.VMEM((1, size), F32) for size in (slots, slots, width)]
        + [pltpu.SemaphoreType.DMA((6 * width // CHUNK + 6,))],
        input_output_aliases=alias,
        compiler_params=params(),
        cost_estimate=cost(10 * slots * width * inner, 6 * width * (inner + slots)),
        name="expert_rows",
    )(first, gates, incoming, w_gate, w_up, w_down, back)


def add_across(value, bit):
    count = lax.axis_size("grp") * lax.axis_size("seq")
    return value + lax.ppermute(value, AXES, [(i, i ^ bit) for i in range(count)])


def query_part(scale, parity, keys, values, grad, prior):
    tok, width = keys.shape

    def work(_, h, at, ins, outs):
        k_ref, v_ref, g_ref, prior_ref = ins
        row, col = triangle(tok)
        g = g_ref[:, at]
        mix_a = jnp.where(row >= col, mm(g, v_ref[:, at], NT), 0.0).astype(BF16)
        outs[0][:, at] = (scale * (mm(mix_a, k_ref[:, at]) + mm(g, prior_ref[h], NT))).astype(BF16)

    outs = [jax.ShapeDtypeStruct((tok, width), BF16)]
    return streamed(work, "query_attention", parity, [keys, values, grad, prior], outs)


def local_part(parity, queries, values, grad, mix):
    tok, width = queries.shape

    def work(_, h, at, ins, outs):
        q_ref, v_ref, g_ref, mix_ref = ins
        row, col = triangle(tok)
        g = g_ref[:, at]
        mix_t = jnp.where(row <= col, mm(v_ref[:, at], g, NT), 0.0).astype(BF16)
        outs[0][:, at] = mm(mix_t, q_ref[:, at]).astype(BF16)
        outs[1][:, at] = mm(mix_ref[:, at], g).astype(BF16)

    outs = [jax.ShapeDtypeStruct((tok, width), BF16)] * 2
    return streamed(work, "local_attention", parity, [queries, values, grad, mix], outs)


def last_part(scale, parity, keys, values, pk, pv, own, other):
    tok, width = keys.shape
    half = own.shape[0]

    def work(parity_ref, h, at, ins, outs):
        k_ref, v_ref, pk_ref, pv_ref, own_ref, other_ref = ins
        gk_ref, gv_ref = outs
        later = jnp.where(parity_ref[0] == h // half, own_ref[h % half], other_ref[h % half])
        gk_ref[:, at] = (scale * (pk_ref[:, at].astype(F32) + mm(v_ref[:, at], later, NT))).astype(BF16)
        gv_ref[:, at] = (scale * (pv_ref[:, at].astype(F32) + mm(k_ref[:, at], later))).astype(BF16)

    outs = [jax.ShapeDtypeStruct((tok, width), BF16)] * 2
    return streamed(work, "last_attention", parity, [keys, values, pk, pv, own, other], outs)


def states_beyond(place, mine, other, beside):
    count = lax.axis_size("seq")
    parity = place & 1

    def swap(value, bit):
        return lax.ppermute(value.astype(BF16), "seq", [(i, i ^ bit) for i in range(count)])

    bits = [1 << b for b in range(1, count.bit_length() - 1)]
    quarter = mine.shape[0] // 2
    partner = swap(other, 1).astype(F32)
    mine = mine.astype(F32)
    both = mine + partner
    rising_sum, falling_base = both[:quarter], both[quarter:]
    rising = jnp.zeros_like(rising_sum)
    falling = jnp.zeros_like(falling_base)
    beside_out = []
    for up, down in zip(bits, reversed(bits)):
        got_up = swap(rising_sum, up)
        got_down = swap(falling + jnp.where((place & down) == 0, 0.0, falling_base), down)
        if beside:
            got_up, got_down, done = lax.optimization_barrier((got_up, got_down, beside.pop(0)(rising_sum)))
            beside_out.append(done)
        got_up, got_down = got_up.astype(F32), got_down.astype(F32)
        rising = rising + jnp.where((place & up) == 0, got_up, 0.0)
        rising_sum = rising_sum + got_up
        falling = falling + got_down
    own = jnp.concatenate([rising, falling])
    theirs = swap(own + jnp.where(parity == 1, mine, 0.0), 1)
    own = (own + jnp.where(parity == 0, partner, 0.0)).astype(BF16)
    return own, theirs, beside_out + [work(rising_sum) for work in beside]


def body(
    stream,
    cotangent,
    norm_gain,
    queries,
    key_vectors,
    value_vectors,
    expert_index,
    router_gates,
    gate_proj,
    up_proj,
    down_proj,
):
    tok, width = stream.shape
    seq_count = lax.axis_size("seq")
    dev_count = seq_count * lax.axis_size("grp")
    experts, capacity = expert_index.shape
    most = 2 * capacity // dev_count
    here = lax.axis_index("grp") * seq_count + lax.axis_index("seq")
    scale = 1.0 / math.sqrt(HEAD * tok * seq_count)
    gain = norm_gain[None, :]
    w_gate, w_up, w_down = gate_proj[0], up_proj[0], down_proj[0]

    halves = dev_count // 2
    swap = [(i, (i + halves) % dev_count) for i in range(dev_count)]
    groups = [[side * halves + i for i in range(halves)] for side in range(2)]
    side = here // halves
    side_array = side.astype(jnp.int32)[None]
    parity = (lax.axis_index("seq") & 1).astype(jnp.int32)[None]
    here_array = here.astype(jnp.int32)[None]
    there_array = ((here + halves) % dev_count).astype(jnp.int32)[None]

    def exchange(value):
        return lax.all_to_all(value, AXES, split_axis=0, concat_axis=0, tiled=True, axis_index_groups=groups)

    inputs, out_own = prepare(most, side_array, here_array, expert_index, gain, cotangent, stream)
    own = exchange(out_own)
    far_cot = lax.ppermute(cotangent, AXES, swap)
    far_inputs = lax.ppermute(inputs, AXES, swap)

    pick_t = picks(most, tok, here_array, expert_index).T
    half_index = lax.dynamic_slice_in_dim(expert_index, side * (experts // 2), experts // 2, 0)
    far_pick = picks(most, tok, there_array, half_index)
    own_index = lax.dynamic_index_in_dim(expert_index, here, 0, keepdims=False)
    source = own_index // tok
    ahead = (source[None, :] == source[:, None]) & (own_index[None, :] < own_index[:, None])
    before = jnp.sum(ahead.astype(jnp.int32), axis=1)
    arrival = jnp.where(source // halves == side, source % halves, halves + source % halves) * most + before
    place_t = arrival[None, :] == jnp.arange(dev_count * most)[:, None]
    slot_gates = jnp.sum(jnp.where(place_t, router_gates, 0.0), axis=1).reshape(2, 1, halves * most)
    far_out = pack(far_pick, far_cot, 1)
    far_inputs, far_out, pick_t, slot_gates = lax.optimization_barrier((far_inputs, far_out, pick_t, slot_gates))
    far_out = pack(far_pick, far_inputs, 0, far_out)
    far = exchange(far_out)

    own, far_out, q_early, k_early, v_early = lax.optimization_barrier(
        (own, far_out, queries, key_vectors, value_vectors)
    )
    key_mine, key_other, mix_b = early(parity, q_early, k_early, v_early)
    back, own_ggp, own_gup, own_hidden, own_router, own_gain = expert(
        side_array, slot_gates[0], own, w_gate, w_up, w_down
    )
    far, back, key_mine, key_other, mix_b = lax.optimization_barrier((far, back, key_mine, key_other, mix_b))
    back, far_ggp, far_gup, far_hidden, far_router, far_gain = expert(
        1 - side_array, slot_gates[1], far, w_gate, w_up, w_down, back
    )
    returned = lax.all_to_all(back, AXES, split_axis=0, concat_axis=0, tiled=True)

    place = lax.axis_index("seq")
    own_prior, other_prior, _ = states_beyond(seq_count - 1 - place, key_mine, key_other, [])
    is_low = parity[0] == 0
    prior = jnp.concatenate(
        [jnp.where(is_low, own_prior, other_prior), jnp.where(is_low, other_prior, own_prior)]
    )
    own, far, far_ggp, back = lax.optimization_barrier((own, far, far_ggp, back))
    arrived = jnp.concatenate([own, far])
    arrived, own_gain, far_gain = lax.optimization_barrier((arrived, own_gain, far_gain))
    gain_total = (own_gain + far_gain) / gain
    bits = [1 << b for b in range(dev_count.bit_length() - 1)]
    for bit in bits[:-2]:
        gain_total = add_across(gain_total, bit)
    rows, dy_rows = arrived[:, :width], arrived[:, width:]
    grad_gate_pre = jnp.concatenate([own_ggp, far_ggp])
    grad_up_pre = jnp.concatenate([own_gup, far_gup])
    hidden = jnp.concatenate([own_hidden, far_hidden])
    grad_gate = lax.dot_general(rows, grad_gate_pre, TN, preferred_element_type=F32).astype(BF16)
    grad_up = lax.dot_general(rows, grad_up_pre, TN, preferred_element_type=F32).astype(BF16)
    grad_down = lax.dot_general(hidden, dy_rows, TN, preferred_element_type=F32).astype(BF16)
    slot_router = jnp.concatenate([own_router, far_router], axis=1).reshape(dev_count * most, 1)
    router = jnp.sum(jnp.where(place_t, slot_router, 0.0), axis=0, keepdims=True)
    returned, grad_gate, grad_up, grad_down, router, gain_total, prior, mix_b = lax.optimization_barrier(
        (returned, grad_gate, grad_up, grad_down, router, gain_total, prior, mix_b)
    )

    grad_stream, mine, other = combine(parity, pick_t, gain, stream, returned, cotangent, queries)

    gain_across = [(i, i ^ bits[-1]) for i in range(dev_count)]
    gain_sums = [gain_total]

    def first(_):
        gain_sums.append(add_across(gain_total, bits[-2]))
        return local_part(parity, queries, value_vectors, grad_stream, mix_b), gain_sums[-1]

    def second(after):
        grad, _ = lax.optimization_barrier((grad_stream, after))
        done = query_part(scale, parity, key_vectors, value_vectors, grad, prior)
        return done, lax.ppermute(gain_sums[-1], AXES, gain_across)

    own_state, other_state, done = states_beyond(place, mine, other, [first, second])
    ((part_k, part_v), gain_total), ((grad_queries,), gain_other) = done
    gain_total += gain_other
    grad_keys, grad_values = last_part(
        scale, parity, key_vectors, value_vectors, part_k, part_v, own_state, other_state
    )
    return (
        grad_stream,
        grad_queries,
        grad_keys,
        grad_values,
        grad_gate[None],
        grad_up[None],
        grad_down[None],
        router,
        gain_total[0],
    )


def solution(mesh):
    rows = P(AXES, None)
    cube = P(AXES, None, None)
    in_specs = (rows, rows, P(), rows, rows, rows, P(), rows, cube, cube, cube)
    out_specs = (rows, rows, rows, rows, cube, cube, cube, rows, P())
    return jax.shard_map(body, mesh=mesh, in_specs=in_specs, out_specs=out_specs, check_vma=False)
```
